32 devices in a mesh: col: 16 (over z, x, core), row: 2 (over y).
Axes of the slice: x: 2, y: 2, z: 4, core: 2. Of those that a mesh axis runs over, the one named last changes fastest.
Arguments:
- matrix: float32 [8, 256, 1, 2048], P(None, 'row', None, 'col'), may hold values from -1 to 5, as said below
- inverse_factors: float32 [2, 512, 512], replicated, may hold values from -1 to 1, as said below
Outputs:
- factored: float32 [8, 256, 1, 2048], P(None, 'row', None, 'col')
The draws below stay inside these ranges and needn't reach their ends.
Inputs may be any that keep to these rules, and one draw needn't show every extreme that they name: matrix holds a symmetric matrix. Each inverse_factors[k] is lower triangular with a positive diagonal; it is given independently of matrix.
All inputs are finite; a program needn't handle non-finite values.
Results may differ from the reference program's by a relative error of at most 0.0001.
Values sent between devices are 32-bit elements; how exact they have to be, the bound alone decides.
A program may use at most 64 MiB of HBM per device.

```python
import jax
import jax.numpy as jnp
from jax import lax

NB = 128
P_SIZE = 512
CYC = 1
M = 2048
N_ROW = 2


def draw_matrix(key, part):
    first_key, second_key = jax.random.split(jax.random.fold_in(key, 17))
    noise = jax.random.normal(first_key, (M, M), jnp.float32)
    square = 0.05 * (noise + noise.T)
    diagonal = 2.0 + 2.0 * jax.random.uniform(second_key, (M,), jnp.float32)
    positions = jnp.arange(M)
    square = square.at[positions, positions].add(diagonal)
    return square.reshape(M // (N_ROW * NB), N_ROW * NB, CYC, M // CYC)


def draw_inverse_factors(key, part):
    first_key, second_key = jax.random.split(jax.random.fold_in(key, 29))
    indices = jnp.arange(P_SIZE)
    diag_values = 1.0 / jnp.sqrt(2.0 + 2.0 * jax.random.uniform(second_key, (2, P_SIZE), jnp.float32))
    noise = jax.random.normal(first_key, (2, P_SIZE, P_SIZE), jnp.float32)
    strict = indices[:, None] > indices[None, :]
    equal = indices[:, None] == indices[None, :]
    below = jnp.where(strict[None], 0.2 * noise / P_SIZE ** 0.5, 0.0)
    return below + jnp.where(equal[None], diag_values[:, :, None], 0.0)


def setup_inputs(seed: int = 0) -> dict:
    arg_keys = jax.random.split(jax.random.key(seed), 3)
    return {
        "matrix": draw_matrix(jax.random.fold_in(arg_keys[2], 71), 0),
        "inverse_factors": draw_inverse_factors(jax.random.fold_in(arg_keys[2], 71), 0),
    }


def exact_dot(left_side, right_side):
    return jnp.dot(left_side, right_side, precision=lax.Precision.HIGHEST, preferred_element_type=jnp.float32)


def reference(matrix, inverse_factors):
    square = matrix.reshape(M, M)
    indices = jnp.arange(M)[:, None]
    for panel in range(2):
        offset = panel * P_SIZE
        factor_cols = exact_dot(square[:, offset:offset + P_SIZE], inverse_factors[panel].T)
        trailing = jnp.where(indices >= offset + P_SIZE, factor_cols, 0.0)
        square = square - exact_dot(trailing, trailing.T)
        square = square.at[:, offset:offset + P_SIZE].set(jnp.where(indices >= offset, factor_cols, 0.0))
    return square.reshape(matrix.shape)
```

```python
import jax
import jax.numpy as jnp
from jax import lax
from jax.experimental import pallas as pl
from jax.experimental.pallas import tpu as pltpu
from jax.sharding import PartitionSpec as P


def broadcast(x, axis, root):
    mine = lax.axis_index(axis) == root
    return lax.psum(jnp.where(mine, x, jnp.zeros_like(x)), axis)


def exact_dot(left_side, right_side):
    return jnp.dot(
        left_side, right_side, precision=lax.Precision.HIGHEST, preferred_element_type=jnp.float32
    )


def shards(matrix, inverse_factors):
    col_count = lax.axis_size("col")
    row_count = lax.axis_size("row")
    col_index = lax.axis_index("col")
    row_index = lax.axis_index("row")
    row_blocks, block_cols, cycles, _ = matrix.shape
    panel_width = inverse_factors.shape[1]
    per_panel = panel_width // block_cols
    local_rows = row_blocks * block_cols
    square_view = matrix.reshape(local_rows, cycles * block_cols)
    global_rows = (
        (jnp.arange(row_blocks)[:, None] * row_count + row_index) * block_cols
        + jnp.arange(block_cols)[None, :]
    ).reshape(-1)
    take_index = (jnp.arange(cycles) * col_count + col_index) // row_count
    row_root = col_index % row_count

    def masked(factor_cols, offset):
        return jnp.where(global_rows[:, None] >= offset, factor_cols, 0.0)

    current = square_view
    for panel in range(2):
        factor = inverse_factors[panel]
        pieces = [
            broadcast(current, "col", panel * per_panel + member) for member in range(per_panel)
        ]
        factor_cols = exact_dot(jnp.concatenate(pieces, axis=1), factor.T)
        trailing = masked(factor_cols, (panel + 1) * panel_width)
        blocked = trailing.reshape(row_blocks, block_cols, panel_width)
        picked = jnp.take(blocked, take_index, axis=0).reshape(cycles * block_cols, panel_width)
        gathered = lax.all_gather(picked, "row", axis=0, tiled=True)
        column_part = lax.dynamic_slice_in_dim(
            gathered, row_root * picked.shape[0], picked.shape[0], 0
        )
        current = current - exact_dot(trailing, column_part.T)
        place_factor_cols = masked(factor_cols, panel * panel_width)
        offset_id = col_index - panel * per_panel
        inside = (offset_id >= 0) & (offset_id < per_panel)
        position = jnp.clip(offset_id, 0, per_panel - 1)
        chosen = lax.dynamic_slice_in_dim(place_factor_cols, position * block_cols, block_cols, 1)
        leading = jnp.where(inside, chosen, current)
        current = jnp.concatenate([leading, current[:, block_cols:]], axis=1)
    return current.reshape(row_blocks, block_cols, cycles, block_cols)


def split(value):
    high = value.astype(jnp.bfloat16)
    return high, (value - high.astype(jnp.float32)).astype(jnp.bfloat16)


def dot3(left_side, right_side, right_dim=0):
    left_high, left_low = split(left_side)
    right_high, right_low = split(right_side)

    def part(left, right):
        return lax.dot_general(
            left, right, (((1,), (right_dim,)), ((), ())), preferred_element_type=jnp.float32
        )

    return part(left_high, right_high) + (part(left_high, right_low) + part(left_low, right_high))


def kernel(
    mat, fac, out, pan, oth, colo, colf, cross, gram, first, second,
    recv, oth_recv, col_recv, up_sem, side_sem, mate_sem, peer_sem, col_sem,
):
    c = lax.axis_index("col")
    r = lax.axis_index("row")
    z = c // 4
    x = (c // 2) % 2
    k = c % 2
    own = c % 4
    beside = own + 2 - 4 * x
    near = own + 1 - 2 * k
    far = beside + 1 - 2 * k
    up = {"col": c + 4, "row": r}
    down = {"col": c - 4, "row": r}
    side = {"col": c + 2 - 4 * x, "row": r}
    mate = {"col": c + 1 - 2 * k, "row": r}
    peer = {"col": c, "row": 1 - r}
    block = mat.shape[1]
    width = fac.shape[1]
    mesh_ids = pl.DeviceIdType.MESH

    def greet(device):
        pl.semaphore_signal(barrier, inc=1, device_id=device, device_id_type=mesh_ids)

    def copy(src, dst, send, receive, device):
        return pltpu.make_async_remote_copy(
            src_ref=src, dst_ref=dst, send_sem=send, recv_sem=receive,
            device_id=device, device_id_type=mesh_ids,
        )

    def active(q, j):
        if q == 0:
            return z == 0 if j == 0 else z >= 0
        return z == 1 if j == 1 else z >= 1

    def rises(q, j):
        return z < 3 if q == 0 else (z >= 1) & (z < 3)

    def climbs(q, j):
        return j >= 1 + q

    def strip(q, s, j):
        return pan.at[q, s, pl.ds(2 * j, 2)]

    def strip_copy(q, s, j, send, device):
        return copy(strip(q, s, j), strip(q, s, j), send, recv.at[q, s, j], device)

    def up_copy(q, j):
        return strip_copy(q, own, j, up_sem.at[q, j], up)

    def side_copy(q, j):
        return strip_copy(q, own, j, side_sem.at[q, j], side)

    def mate_copy(q, j, which):
        return strip_copy(q, (own, beside)[which], j, mate_sem.at[q, j, which], mate)

    def arrived(q, s, j):
        strip_copy(q, s, j, up_sem.at[q, j], mate).wait_recv()

    def peer_copy(which):
        s = (own, beside)[which]
        return copy(strip(0, s, 1), oth.at[s], peer_sem.at[0, which], oth_recv.at[s], peer)

    def oth_copy(which):
        s = (own, beside)[which]
        return copy(oth.at[s], oth.at[s], peer_sem.at[1, which], oth_recv.at[s], mate)

    def oth_arrived(s):
        copy(oth.at[s], oth.at[s], peer_sem.at[1, 0], oth_recv.at[s], mate).wait_recv()

    col_copy = copy(mat.at[pl.ds(0, 4)], colo, col_sem, col_recv, peer)

    def lane(q, j):
        @pl.when(active(q, j))
        def _():
            @pl.when(z != q)
            def _():
                arrived(q, own, j)

            if climbs(q, j):
                @pl.when(rises(q, j))
                def _():
                    up_copy(q, j).start()

            side_copy(q, j).start()
            mate_copy(q, j, 0).start()

    def across(q, j):
        @pl.when(active(q, j))
        def _():
            arrived(q, beside, j)
            mate_copy(q, j, 1).start()

    def complete(q, j):
        @pl.when(active(q, j))
        def _():
            arrived(q, near, j)
            arrived(q, far, j)

    def rows(q, j):
        half = [
            jnp.concatenate([pan[q, s, 2 * j + i] for s in range(4)], axis=1) for i in range(2)
        ]
        return jnp.concatenate(half, axis=0)

    def put(j, value):
        out[2 * j] = value[:block]
        out[2 * j + 1] = value[block:]

    def base(j):
        return jnp.concatenate([mat[2 * j], mat[2 * j + 1]], axis=0)

    barrier = pltpu.get_barrier_semaphore()
    greet(side)
    greet(mate)
    greet(peer)

    @pl.when(z < 3)
    def _():
        greet(up)

    @pl.when(z > 0)
    def _():
        greet(down)

    for q in range(2):
        @pl.when(z == q)
        def _():
            pan[q, own] = mat[...]

    between = (z > 0) & (z < 3)

    @pl.when(between)
    def _():
        pl.semaphore_wait(barrier, 5)

    @pl.when(jnp.logical_not(between))
    def _():
        pl.semaphore_wait(barrier, 4)

    chunks = [(1, 2), (0, 1), (1, 3), (0, 2), (0, 3), (1, 1), (0, 0)]

    @pl.when(z == 1)
    def _():
        lane(1, 2)

    @pl.when(z == 0)
    def _():
        lane(0, 1)
        lane(0, 2)
        lane(0, 0)
        lane(0, 3)

    @pl.when(z >= 2)
    def _():
        col_copy.start()

    @pl.when(z >= 1)
    def _():
        gram[0] = dot3(fac[0].T, fac[0])

    @pl.when(z >= 2)
    def _():
        gram[1] = dot3(fac[1].T, fac[1])

    @pl.when(z >= 1)
    def _():
        lane(0, 1)
        peer_copy(0).start()

        @pl.when(z >= 2)
        def _():
            lane(1, 2)

        across(0, 1)
        peer_copy(1).start()
        lane(1, 3)
        across(1, 2)
        oth_arrived(own)
        oth_copy(0).start()
        lane(0, 2)
        lane(1, 1)
        across(1, 3)

        @pl.when(z >= 2)
        def _():
            col_copy.wait_recv()
            for i in range(4):
                colf[2 * i + r] = mat[i]
                colf[2 * i + 1 - r] = colo[i]
            first[...] = dot3(gram[0], colf[0:4].reshape(width, block))

        oth_arrived(beside)
        oth_copy(1).start()
        across(0, 2)
        lane(0, 3)
        across(1, 1)
        across(0, 3)

        complete(0, 1)
        oth_arrived(near)
        oth_arrived(far)
        for i in range(2):
            for s in range(4):
                cross[2 * i + r, :, s * block:(s + 1) * block] = pan[0, s, 2 + i]
                cross[2 * i + 1 - r, :, s * block:(s + 1) * block] = oth[s, i]

        @pl.when(z == 1)
        def _():
            second[...] = -fac[1, pl.ds(pl.multiple_of(own * block, block), block), :].T
            first[...] = -dot3(cross[...].reshape(width, width).T, second[...])

        @pl.when(z >= 2)
        def _():
            put(0, base(0))
            lower = dot3(cross[...].reshape(width, width), first[...])
            colf[4:8] = colf[4:8] - lower.reshape(4, block, block)
            for i in range(2):
                out[2 + i] = colf[4 + 2 * i + r]
            second[...] = dot3(gram[1], colf[4:8].reshape(width, block))
            first[...] = colf[0:4].reshape(width, block) - dot3(
                cross[...].reshape(width, width).T, second[...]
            )

        first[...] = dot3(gram[0], first[...])
        first_value, second_value = first[...], second[...]

        @pl.when(z == 1)
        def _():
            put(0, jnp.zeros((2 * block, block), jnp.float32))
            complete(1, 1)
            put(1, -(dot3(rows(0, 1), first[...]) + dot3(rows(1, 1), second[...])))

        for j in (2, 3):
            complete(1, j)
            complete(0, j)
            update = dot3(rows(1, j), second_value) + dot3(rows(0, j), first_value)
            put(j, jnp.where(z >= 2, base(j), 0.0) - update)

    @pl.when(z == 0)
    def _():
        for j in (1, 2, 0, 3):
            across(0, j)
        factor = fac[0, pl.ds(pl.multiple_of(own * block, block), block), :]
        for j in (1, 2, 0, 3):
            complete(0, j)
            put(j, dot3(rows(0, j), factor, 1))

    for q, j in chunks:
        @pl.when(active(q, j))
        def _():
            if climbs(q, j):
                @pl.when(rises(q, j))
                def _():
                    up_copy(q, j).wait_send()
            side_copy(q, j).wait_send()
            mate_copy(q, j, 0).wait_send()
            mate_copy(q, j, 1).wait_send()

    @pl.when(z >= 1)
    def _():
        for which in range(2):
            peer_copy(which).wait_send()
            oth_copy(which).wait_send()

    @pl.when(z >= 2)
    def _():
        col_copy.wait_send()


def panels(matrix, inverse_factors):
    row_blocks, block, _, _ = matrix.shape
    width = inverse_factors.shape[1]
    square = pltpu.VMEM((width, block), jnp.float32)
    dma = pltpu.SemaphoreType.DMA
    vmem = pl.BlockSpec(memory_space=pltpu.VMEM)
    result = pl.pallas_call(
        kernel,
        out_shape=jax.ShapeDtypeStruct((row_blocks, block, block), jnp.float32),
        in_specs=[vmem, vmem],
        out_specs=vmem,
        scratch_shapes=[
            pltpu.VMEM((2, 4, row_blocks, block, block), jnp.float32),
            pltpu.VMEM((4, 2, block, block), jnp.float32),
            pltpu.VMEM((4, block, block), jnp.float32),
            pltpu.VMEM((8, block, block), jnp.float32),
            pltpu.VMEM((4, block, width), jnp.float32),
            pltpu.VMEM((2, width, width), jnp.float32),
            square,
            square,
            dma((2, 4, 4)),
            dma((4,)),
            dma,
            dma((2, 4)),
            dma((2, 4)),
            dma((2, 4, 2)),
            dma((2, 2)),
            dma,
        ],
        compiler_params=pltpu.CompilerParams(
            collective_id=0, has_side_effects=True, vmem_limit_bytes=48 * 1024 * 1024
        ),
        cost_estimate=pl.CostEstimate(
            flops=2 * 10**9, bytes_accessed=4 * 2**20, transcendentals=0
        ),
    )(matrix.reshape(row_blocks, block, block), inverse_factors)
    return result.reshape(matrix.shape)


def solution(mesh):
    small = mesh.shape["col"] == 16 and mesh.shape["row"] == 2
    return jax.shard_map(
        panels if small else shards,
        mesh=mesh,
        in_specs=(P(None, "row", None, "col"), P()),
        out_specs=P(None, "row", None, "col"),
        check_vma=False,
    )
```

```python
import jax
import jax.numpy as jnp
from jax import lax
from jax.experimental import pallas as pl
from jax.experimental.pallas import tpu as pltpu
from jax.sharding import PartitionSpec as P


def broadcast(x, axis, root):
    mine = lax.axis_index(axis) == root
    return lax.psum(jnp.where(mine, x, jnp.zeros_like(x)), axis)


def exact_dot(left_side, right_side):
    return jnp.dot(
        left_side, right_side, precision=lax.Precision.HIGHEST, preferred_element_type=jnp.float32
    )


def shards(matrix, inverse_factors):
    col_count = lax.axis_size("col")
    row_count = lax.axis_size("row")
    col_index = lax.axis_index("col")
    row_index = lax.axis_index("row")
    row_blocks, block_cols, cycles, _ = matrix.shape
    panel_width = inverse_factors.shape[1]
    per_panel = panel_width // block_cols
    local_rows = row_blocks * block_cols
    square_view = matrix.reshape(local_rows, cycles * block_cols)
    global_rows = (
        (jnp.arange(row_blocks)[:, None] * row_count + row_index) * block_cols
        + jnp.arange(block_cols)[None, :]
    ).reshape(-1)
    take_index = (jnp.arange(cycles) * col_count + col_index) // row_count
    row_root = col_index % row_count

    def masked(factor_cols, offset):
        return jnp.where(global_rows[:, None] >= offset, factor_cols, 0.0)

    current = square_view
    for panel in range(2):
        factor = inverse_factors[panel]
        pieces = [
            broadcast(current, "col", panel * per_panel + member) for member in range(per_panel)
        ]
        factor_cols = exact_dot(jnp.concatenate(pieces, axis=1), factor.T)
        trailing = masked(factor_cols, (panel + 1) * panel_width)
        blocked = trailing.reshape(row_blocks, block_cols, panel_width)
        picked = jnp.take(blocked, take_index, axis=0).reshape(cycles * block_cols, panel_width)
        gathered = lax.all_gather(picked, "row", axis=0, tiled=True)
        column_part = lax.dynamic_slice_in_dim(
            gathered, row_root * picked.shape[0], picked.shape[0], 0
        )
        current = current - exact_dot(trailing, column_part.T)
        place_factor_cols = masked(factor_cols, panel * panel_width)
        offset_id = col_index - panel * per_panel
        inside = (offset_id >= 0) & (offset_id < per_panel)
        position = jnp.clip(offset_id, 0, per_panel - 1)
        chosen = lax.dynamic_slice_in_dim(place_factor_cols, position * block_cols, block_cols, 1)
        leading = jnp.where(inside, chosen, current)
        current = jnp.concatenate([leading, current[:, block_cols:]], axis=1)
    return current.reshape(row_blocks, block_cols, cycles, block_cols)


def split(value):
    high = value.astype(jnp.bfloat16)
    return high, (value - high.astype(jnp.float32)).astype(jnp.bfloat16)


def dot3(left_side, right_side, right_dim=0):
    left_high, left_low = split(left_side)
    right_high, right_low = split(right_side)

    def part(left, right):
        return lax.dot_general(
            left, right, (((1,), (right_dim,)), ((), ())), preferred_element_type=jnp.float32
        )

    return part(left_high, right_high) + (part(left_high, right_low) + part(left_low, right_high))


def kernel(
    mat, fac, out, pan, oth, colf, dcol, cross, gram, first, second,
    recv, oth_recv, col_recv, up_sem, side_sem, mate_sem, peer_sem, col_sem, strip_recv, strip_send,
):
    c = lax.axis_index("col")
    r = lax.axis_index("row")
    z = c // 4
    x = (c // 2) % 2
    k = c % 2
    own = c % 4
    beside = own + 2 - 4 * x
    near = own + 1 - 2 * k
    far = beside + 1 - 2 * k
    up = {"col": c + 4, "row": r}
    down = {"col": c - 4, "row": r}
    side = {"col": c + 2 - 4 * x, "row": r}
    mate = {"col": c + 1 - 2 * k, "row": r}
    peer = {"col": c, "row": 1 - r}
    block = mat.shape[1]
    width = fac.shape[1]
    mesh_ids = pl.DeviceIdType.MESH

    def greet(device):
        pl.semaphore_signal(barrier, inc=1, device_id=device, device_id_type=mesh_ids)

    def copy(src, dst, send, receive, device):
        return pltpu.make_async_remote_copy(
            src_ref=src, dst_ref=dst, send_sem=send, recv_sem=receive,
            device_id=device, device_id_type=mesh_ids,
        )

    def active(q, j):
        if q == 0:
            return (z == 0, z >= 0, z < 2, z < 2)[j]
        return z == 1

    def rises(q, j):
        return z < 3 if j == 1 else z == 0

    def climbs(q, j):
        return q == 0 and j >= 1

    def strip(q, s, j):
        return pan.at[q, s, pl.ds(2 * j, 2)]

    def strip_copy(q, s, j, send, device):
        return copy(strip(q, s, j), strip(q, s, j), send, recv.at[q, s, j], device)

    def up_copy(q, j):
        return strip_copy(q, own, j, up_sem.at[q, j], up)

    def side_copy(q, j):
        return strip_copy(q, own, j, side_sem.at[q, j], side)

    def mate_copy(q, j, which):
        return strip_copy(q, (own, beside)[which], j, mate_sem.at[q, j, which], mate)

    def arrived(q, s, j):
        strip_copy(q, s, j, up_sem.at[q, j], mate).wait_recv()

    def peer_copy(which):
        s = (own, beside)[which]
        return copy(strip(0, s, 1), oth.at[s], peer_sem.at[0, which], oth_recv.at[s], peer)

    def oth_copy(which):
        s = (own, beside)[which]
        return copy(oth.at[s], oth.at[s], peer_sem.at[1, which], oth_recv.at[s], mate)

    def oth_arrived(s):
        copy(oth.at[s], oth.at[s], peer_sem.at[1, 0], oth_recv.at[s], mate).wait_recv()

    def col_copy(i):
        return copy(mat.at[i], colf.at[2 * i + r], col_sem.at[i], col_recv.at[i], peer)

    turn = 4 * (5 - 2 * z)
    turned = {"col": c + turn, "row": r}
    here = (z - 2) * 2 + x
    over = here + 1 - 2 * x
    ahead = here + turn // 2
    slots = (here, over, ahead, over + turn // 2)

    def place(m):
        return 2 * m + r if m < 4 else 2 * (m - 4) + 1 - r

    def strip_send_copy(slot, m, way):
        device = (side, turned, mate)[way]
        p = place(m)
        src = colf.at[p] if slot == 0 else dcol.at[slots[slot], p]
        return copy(
            src, dcol.at[slots[slot], p], strip_send.at[slot, m, way],
            strip_recv.at[slots[slot], p], device,
        )

    def strip_wait(g, p):
        copy(
            dcol.at[g, p], dcol.at[g, p], strip_send.at[0, 0, 0], strip_recv.at[g, p], mate
        ).wait_recv()

    def ways(slot, m):
        if slot == 0:
            return (0, 1, 2)
        if slot == 1:
            return (1, 2) if m % 4 < 2 else (2,)
        if slot == 2:
            return (2,) if m % 4 < 2 else (0, 2)
        return (2,)

    holder = (z >= 2) & (k == r)

    def hand_on(slot, m):
        if slot > 0:
            strip_wait(slots[slot], place(m))
        for way in ways(slot, m):
            strip_send_copy(slot, m, way).start()

    def lane(q, j):
        @pl.when(active(q, j))
        def _():
            @pl.when(z != q)
            def _():
                arrived(q, own, j)

            if climbs(q, j):
                @pl.when(rises(q, j))
                def _():
                    up_copy(q, j).start()

            side_copy(q, j).start()
            mate_copy(q, j, 0).start()

    def across(q, j):
        @pl.when(active(q, j))
        def _():
            arrived(q, beside, j)
            mate_copy(q, j, 1).start()

    def complete(q, j):
        @pl.when(active(q, j))
        def _():
            arrived(q, near, j)
            arrived(q, far, j)

    def rows(q, j):
        half = [
            jnp.concatenate([pan[q, s, 2 * j + i] for s in range(4)], axis=1) for i in range(2)
        ]
        return jnp.concatenate(half, axis=0)

    def put(j, value):
        out[2 * j] = value[:block]
        out[2 * j + 1] = value[block:]

    def base(j):
        return jnp.concatenate([mat[2 * j], mat[2 * j + 1]], axis=0)

    @pl.when(z >= 2)
    def _():
        for i in range(4):
            colf[2 * i + r] = mat[i]

    barrier = pltpu.get_barrier_semaphore()
    greet(side)
    greet(mate)
    greet(peer)

    @pl.when(z < 3)
    def _():
        greet(up)

    @pl.when(z > 0)
    def _():
        greet(down)

    for q in range(2):
        @pl.when(z == q)
        def _():
            pan[q, own] = mat[...]

    between = (z > 0) & (z < 3)

    @pl.when(between)
    def _():
        pl.semaphore_wait(barrier, 5)

    @pl.when(jnp.logical_not(between))
    def _():
        pl.semaphore_wait(barrier, 4)

    chunks = [(1, 2), (0, 1), (1, 3), (0, 2), (0, 3), (1, 1), (0, 0)]

    @pl.when(z == 1)
    def _():
        lane(1, 2)
        lane(1, 3)
        lane(1, 1)

    @pl.when(z == 0)
    def _():
        lane(0, 1)
        lane(0, 2)
        lane(0, 0)
        lane(0, 3)

    @pl.when(z >= 2)
    def _():
        for i in range(4):
            col_copy(i).start()

    @pl.when(holder)
    def _():
        for m in range(4):
            hand_on(0, m)

    @pl.when(z >= 1)
    def _():
        gram[0] = dot3(fac[0].T, fac[0])
        lane(0, 1)
        peer_copy(0).start()

        @pl.when(z >= 2)
        def _():
            for i in range(4):
                copy(
                    mat.at[i], colf.at[2 * i + 1 - r], col_sem.at[i], col_recv.at[i], peer
                ).wait_recv()

        @pl.when(holder)
        def _():
            for m in range(4, 8):
                hand_on(0, m)

        across(0, 1)
        peer_copy(1).start()

        @pl.when(z == 1)
        def _():
            lane(0, 2)

        @pl.when(holder)
        def _():
            for m in range(4):
                hand_on(1, m)
                hand_on(2, m)

        @pl.when(z >= 2)
        def _():
            first[...] = dot3(gram[0], colf[0:4].reshape(width, block))

        oth_arrived(own)
        oth_copy(0).start()

        @pl.when(z == 1)
        def _():
            across(1, 2)
            across(1, 3)
            across(1, 1)
            lane(0, 3)

        oth_arrived(beside)
        oth_copy(1).start()

        @pl.when(z == 1)
        def _():
            across(0, 2)

        @pl.when(holder)
        def _():
            for m in range(4, 8):
                hand_on(1, m)
                hand_on(2, m)
            for m in range(8):
                hand_on(3, m)
            dcol[here] = colf[...]

        @pl.when(z >= 2)
        def _():
            gram[1] = dot3(fac[1].T, fac[1])

        complete(0, 1)
        oth_arrived(near)
        oth_arrived(far)
        for i in range(2):
            for s in range(4):
                cross[2 * i + r, :, s * block:(s + 1) * block] = pan[0, s, 2 + i]
                cross[2 * i + 1 - r, :, s * block:(s + 1) * block] = oth[s, i]

    @pl.when(z == 1)
    def _():
        second[...] = -fac[1, pl.ds(pl.multiple_of(own * block, block), block), :].T
        first[...] = -dot3(cross[...].reshape(width, width).T, second[...])
        first[...] = dot3(gram[0], first[...])
        across(0, 3)
        put(0, jnp.zeros((2 * block, block), jnp.float32))
        for j in (1, 2, 3):
            complete(1, j)
            if j > 1:
                complete(0, j)
            put(j, -(dot3(rows(0, j), first[...]) + dot3(rows(1, j), second[...])))

    @pl.when(z >= 2)
    def _():
        put(0, base(0))
        lower = colf[4:8].reshape(width, block) - dot3(
            cross[...].reshape(width, width), first[...]
        )
        second[...] = lower
        for i in range(2):
            out[2 + i] = second[pl.ds(pl.multiple_of((2 * i + r) * block, block), block), :]
        second[...] = dot3(gram[1], lower)
        first[...] = colf[0:4].reshape(width, block) - dot3(
            cross[...].reshape(width, width).T, second[...]
        )
        first[...] = dot3(gram[0], first[...])

        @pl.when(k != r)
        def _():
            for g in range(4):
                for p in range(8):
                    strip_wait(g, p)

        both = jnp.concatenate([first[...].T, second[...].T], axis=1)
        for pair in range(2):
            strips = jnp.concatenate(
                [dcol[2 * pair + i].reshape(2 * width, block) for i in range(2)], axis=1
            )
            update = dot3(both, strips)
            for i in range(2):
                a = 4 + 2 * pair + i
                out[a] = mat[a] - update[:, i * block:(i + 1) * block].T

    @pl.when(z == 0)
    def _():
        for j in (1, 2, 0, 3):
            across(0, j)
        factor = fac[0, pl.ds(pl.multiple_of(own * block, block), block), :]
        for j in (1, 2, 0, 3):
            complete(0, j)
            put(j, dot3(rows(0, j), factor, 1))

    for q, j in chunks:
        @pl.when(active(q, j))
        def _():
            if climbs(q, j):
                @pl.when(rises(q, j))
                def _():
                    up_copy(q, j).wait_send()
            side_copy(q, j).wait_send()
            mate_copy(q, j, 0).wait_send()
            mate_copy(q, j, 1).wait_send()

    @pl.when(z >= 1)
    def _():
        for which in range(2):
            peer_copy(which).wait_send()
            oth_copy(which).wait_send()

    @pl.when(z >= 2)
    def _():
        for i in range(4):
            col_copy(i).wait_send()

    @pl.when(holder)
    def _():
        for slot in range(4):
            for m in range(8):
                for way in ways(slot, m):
                    strip_send_copy(slot, m, way).wait_send()


def panels(matrix, inverse_factors):
    row_blocks, block, _, _ = matrix.shape
    width = inverse_factors.shape[1]
    square = pltpu.VMEM((width, block), jnp.float32)
    dma = pltpu.SemaphoreType.DMA
    vmem = pl.BlockSpec(memory_space=pltpu.VMEM)
    result = pl.pallas_call(
        kernel,
        out_shape=jax.ShapeDtypeStruct((row_blocks, block, block), jnp.float32),
        in_specs=[vmem, vmem],
        out_specs=vmem,
        scratch_shapes=[
            pltpu.VMEM((2, 4, row_blocks, block, block), jnp.float32),
            pltpu.VMEM((4, 2, block, block), jnp.float32),
            pltpu.VMEM((8, block, block), jnp.float32),
            pltpu.VMEM((4, 8, block, block), jnp.float32),
            pltpu.VMEM((4, block, width), jnp.float32),
            pltpu.VMEM((2, width, width), jnp.float32),
            square,
            square,
            dma((2, 4, 4)),
            dma((4,)),
            dma((4,)),
            dma((2, 4)),
            dma((2, 4)),
            dma((2, 4, 2)),
            dma((2, 2)),
            dma((4,)),
            dma((4, 8)),
            dma((4, 8, 3)),
        ],
        compiler_params=pltpu.CompilerParams(
            collective_id=0, has_side_effects=True, vmem_limit_bytes=48 * 1024 * 1024
        ),
        cost_estimate=pl.CostEstimate(
            flops=2 * 10**9, bytes_accessed=4 * 2**20, transcendentals=0
        ),
    )(matrix.reshape(row_blocks, block, block), inverse_factors)
    return result.reshape(matrix.shape)


def solution(mesh):
    small = mesh.shape["col"] == 16 and mesh.shape["row"] == 2
    return jax.shard_map(
        panels if small else shards,
        mesh=mesh,
        in_specs=(P(None, "row", None, "col"), P()),
        out_specs=P(None, "row", None, "col"),
        check_vma=False,
    )
```

```python
import jax
import jax.numpy as jnp
from jax import lax
from jax.experimental import pallas as pl
from jax.experimental.pallas import tpu as pltpu
from jax.sharding import PartitionSpec as P


def broadcast(x, axis, root):
    mine = lax.axis_index(axis) == root
    return lax.psum(jnp.where(mine, x, jnp.zeros_like(x)), axis)


def exact_dot(left_side, right_side):
    return jnp.dot(
        left_side, right_side, precision=lax.Precision.HIGHEST, preferred_element_type=jnp.float32
    )


def shards(matrix, inverse_factors):
    col_count = lax.axis_size("col")
    row_count = lax.axis_size("row")
    col_index = lax.axis_index("col")
    row_index = lax.axis_index("row")
    row_blocks, block_cols, cycles, _ = matrix.shape
    panel_width = inverse_factors.shape[1]
    per_panel = panel_width // block_cols
    local_rows = row_blocks * block_cols
    square_view = matrix.reshape(local_rows, cycles * block_cols)
    global_rows = (
        (jnp.arange(row_blocks)[:, None] * row_count + row_index) * block_cols
        + jnp.arange(block_cols)[None, :]
    ).reshape(-1)
    take_index = (jnp.arange(cycles) * col_count + col_index) // row_count
    row_root = col_index % row_count

    def masked(factor_cols, offset):
        return jnp.where(global_rows[:, None] >= offset, factor_cols, 0.0)

    current = square_view
    for panel in range(2):
        factor = inverse_factors[panel]
        pieces = [
            broadcast(current, "col", panel * per_panel + member) for member in range(per_panel)
        ]
        factor_cols = exact_dot(jnp.concatenate(pieces, axis=1), factor.T)
        trailing = masked(factor_cols, (panel + 1) * panel_width)
        blocked = trailing.reshape(row_blocks, block_cols, panel_width)
        picked = jnp.take(blocked, take_index, axis=0).reshape(cycles * block_cols, panel_width)
        gathered = lax.all_gather(picked, "row", axis=0, tiled=True)
        column_part = lax.dynamic_slice_in_dim(
            gathered, row_root * picked.shape[0], picked.shape[0], 0
        )
        current = current - exact_dot(trailing, column_part.T)
        place_factor_cols = masked(factor_cols, panel * panel_width)
        offset_id = col_index - panel * per_panel
        inside = (offset_id >= 0) & (offset_id < per_panel)
        position = jnp.clip(offset_id, 0, per_panel - 1)
        chosen = lax.dynamic_slice_in_dim(place_factor_cols, position * block_cols, block_cols, 1)
        leading = jnp.where(inside, chosen, current)
        current = jnp.concatenate([leading, current[:, block_cols:]], axis=1)
    return current.reshape(row_blocks, block_cols, cycles, block_cols)


def split(value):
    high = value.astype(jnp.bfloat16)
    return high, (value - high.astype(jnp.float32)).astype(jnp.bfloat16)


def dot3(left_side, right_side, right_dim=0):
    left_high, left_low = split(left_side)
    right_high, right_low = split(right_side)

    def part(left, right):
        return lax.dot_general(
            left, right, (((1,), (right_dim,)), ((), ())), preferred_element_type=jnp.float32
        )

    return part(left_high, right_high) + (part(left_high, right_low) + part(left_low, right_high))


def kernel(
    mat_hbm, fac_hbm, out, mat, fac, pan, oth, colf, dcol, cross, gram, first, second,
    recv, oth_recv, col_recv, up_sem, side_sem, mate_sem, peer_sem, col_sem, strip_recv, strip_send, load_sem,
):
    c = lax.axis_index("col")
    r = lax.axis_index("row")
    z = c // 4
    x = (c // 2) % 2
    k = c % 2
    own = c % 4
    beside = own + 2 - 4 * x
    near = own + 1 - 2 * k
    far = beside + 1 - 2 * k
    up = {"col": c + 4, "row": r}
    down = {"col": c - 4, "row": r}
    side = {"col": c + 2 - 4 * x, "row": r}
    mate = {"col": c + 1 - 2 * k, "row": r}
    peer = {"col": c, "row": 1 - r}
    block = mat.shape[1]
    width = fac.shape[1]
    mesh_ids = pl.DeviceIdType.MESH

    def greet(device):
        pl.semaphore_signal(barrier, inc=1, device_id=device, device_id_type=mesh_ids)

    def copy(src, dst, send, receive, device):
        return pltpu.make_async_remote_copy(
            src_ref=src, dst_ref=dst, send_sem=send, recv_sem=receive,
            device_id=device, device_id_type=mesh_ids,
        )

    def active(q, j):
        if q == 0:
            return (z == 0, z >= 0, z < 2, z < 2)[j]
        return z == 1

    def rises(q, j):
        return z < 3 if j == 1 else z == 0

    def climbs(q, j):
        return q == 0 and j >= 1

    def strip(q, s, j):
        return pan.at[q, s, pl.ds(2 * j, 2)]

    def strip_copy(q, s, j, send, device):
        return copy(strip(q, s, j), strip(q, s, j), send, recv.at[q, s, j], device)

    def up_copy(q, j):
        return strip_copy(q, own, j, up_sem.at[q, j], up)

    def side_copy(q, j):
        return strip_copy(q, own, j, side_sem.at[q, j], side)

    def mate_copy(q, j, which):
        return strip_copy(q, (own, beside)[which], j, mate_sem.at[q, j, which], mate)

    def arrived(q, s, j):
        strip_copy(q, s, j, up_sem.at[q, j], mate).wait_recv()

    def peer_copy(which):
        s = (own, beside)[which]
        return copy(strip(0, s, 1), oth.at[s], peer_sem.at[0, which], oth_recv.at[s], peer)

    def oth_copy(which):
        s = (own, beside)[which]
        return copy(oth.at[s], oth.at[s], peer_sem.at[1, which], oth_recv.at[s], mate)

    def oth_arrived(s):
        copy(oth.at[s], oth.at[s], peer_sem.at[1, 0], oth_recv.at[s], mate).wait_recv()

    def col_copy(i):
        return copy(mat.at[i], colf.at[2 * i + r], col_sem.at[i], col_recv.at[i], peer)

    turn = 4 * (5 - 2 * z)
    turned = {"col": c + turn, "row": r}
    here = (z - 2) * 2 + x
    over = here + 1 - 2 * x
    ahead = here + turn // 2
    slots = (here, over, ahead, over + turn // 2)

    def place(m):
        return 2 * m + r if m < 4 else 2 * (m - 4) + 1 - r

    def strip_send_copy(slot, m, way):
        device = (side, turned, mate)[way]
        p = place(m)
        from_column = slot == 0 and (m % 2 == 0 or way == 2)
        src = colf.at[p] if from_column else dcol.at[slots[slot], p]
        return copy(
            src, dcol.at[slots[slot], p], strip_send.at[slot, m, way],
            strip_recv.at[slots[slot], p], device,
        )

    def strip_wait(g, p):
        copy(
            dcol.at[g, p], dcol.at[g, p], strip_send.at[0, 0, 0], strip_recv.at[g, p], mate
        ).wait_recv()

    def ways(slot, m):
        if slot == 0:
            return (0, 1, 2)
        if slot == 1:
            return (1, 2) if m % 4 < 2 else (2,)
        if slot == 2:
            return (2,) if m % 4 < 2 else (0, 2)
        return (2,)

    holder = (z >= 2) & (k == r)
    helper = (z >= 2) & (k != r)

    def carried(cases):
        for even, condition in ((True, holder), (False, helper)):
            @pl.when(condition)
            def _():
                for slot, m in cases:
                    if (m % 2 == 0) == even:
                        hand_on(slot, m)

    def hand_on(slot, m):
        if slot > 0 or m % 2:
            strip_wait(slots[slot], place(m))
        for way in ways(slot, m):
            if slot > 0 or m % 2 == 0 or way < 2:
                strip_send_copy(slot, m, way).start()

    def lane(q, j):
        @pl.when(active(q, j))
        def _():
            @pl.when(z != q)
            def _():
                arrived(q, own, j)

            if climbs(q, j):
                @pl.when(rises(q, j))
                def _():
                    up_copy(q, j).start()

            side_copy(q, j).start()
            mate_copy(q, j, 0).start()

    def across(q, j):
        @pl.when(active(q, j))
        def _():
            arrived(q, beside, j)
            mate_copy(q, j, 1).start()

    def complete(q, j):
        @pl.when(active(q, j))
        def _():
            arrived(q, near, j)
            arrived(q, far, j)

    def rows(q, j):
        half = [
            jnp.concatenate([pan[q, s, 2 * j + i] for s in range(4)], axis=1) for i in range(2)
        ]
        return jnp.concatenate(half, axis=0)

    def put(j, value):
        out[2 * j] = value[:block]
        out[2 * j + 1] = value[block:]

    def base(j):
        return jnp.concatenate([mat[2 * j], mat[2 * j + 1]], axis=0)

    mat_load = pltpu.make_async_copy(mat_hbm, mat, load_sem.at[0])
    fac_load = pltpu.make_async_copy(fac_hbm, fac, load_sem.at[1])
    mat_load.start()
    fac_load.start()

    barrier = pltpu.get_barrier_semaphore()
    greet(side)
    greet(mate)
    greet(peer)

    @pl.when(z < 3)
    def _():
        greet(up)

    @pl.when(z > 0)
    def _():
        greet(down)

    mat_load.wait()

    @pl.when(z >= 2)
    def _():
        for i in range(4):
            colf[2 * i + r] = mat[i]

    for q in range(2):
        @pl.when(z == q)
        def _():
            pan[q, own] = mat[...]

    between = (z > 0) & (z < 3)

    @pl.when(between)
    def _():
        pl.semaphore_wait(barrier, 5)

    @pl.when(jnp.logical_not(between))
    def _():
        pl.semaphore_wait(barrier, 4)

    chunks = [(1, 2), (0, 1), (1, 3), (0, 2), (0, 3), (1, 1), (0, 0)]

    @pl.when(z == 1)
    def _():
        lane(1, 2)
        lane(1, 3)
        lane(1, 1)

    @pl.when(z == 0)
    def _():
        lane(0, 1)
        lane(0, 2)
        lane(0, 0)
        lane(0, 3)

    @pl.when(z >= 2)
    def _():
        for i in range(4):
            col_copy(i).start()

    @pl.when(holder)
    def _():
        for m in (1, 3):
            strip_send_copy(0, m, 2).start()

    carried([(0, m) for m in range(4)])
    fac_load.wait()

    @pl.when(z >= 1)
    def _():
        gram[0] = dot3(fac[0].T, fac[0])
        lane(0, 1)
        peer_copy(0).start()

        @pl.when(z >= 2)
        def _():
            for i in range(4):
                copy(
                    mat.at[i], colf.at[2 * i + 1 - r], col_sem.at[i], col_recv.at[i], peer
                ).wait_recv()

        @pl.when(holder)
        def _():
            for m in (5, 7):
                strip_send_copy(0, m, 2).start()

        carried([(0, m) for m in range(4, 8)])

        across(0, 1)
        peer_copy(1).start()

        @pl.when(z == 1)
        def _():
            lane(0, 2)

        carried([(slot, m) for m in range(4) for slot in (1, 2)])

        @pl.when(z >= 2)
        def _():
            gram[1] = dot3(fac[1].T, fac[1])
            first[...] = dot3(gram[0], colf[0:4].reshape(width, block))

        oth_arrived(own)
        oth_copy(0).start()

        @pl.when(z == 1)
        def _():
            across(1, 2)
            across(1, 3)
            across(1, 1)
            lane(0, 3)

        oth_arrived(beside)
        oth_copy(1).start()

        @pl.when(z == 1)
        def _():
            across(0, 2)

        carried([(slot, m) for m in range(4, 8) for slot in (1, 2)])
        carried([(3, m) for m in range(8)])

        @pl.when(holder)
        def _():
            dcol[here] = colf[...]

        complete(0, 1)
        oth_arrived(near)
        oth_arrived(far)
        for i in range(2):
            for s in range(4):
                cross[2 * i + r, :, s * block:(s + 1) * block] = pan[0, s, 2 + i]
                cross[2 * i + 1 - r, :, s * block:(s + 1) * block] = oth[s, i]

    @pl.when(z == 1)
    def _():
        second[...] = -fac[1, pl.ds(pl.multiple_of(own * block, block), block), :].T
        first[...] = -dot3(cross[...].reshape(width, width).T, second[...])
        first[...] = dot3(gram[0], first[...])
        across(0, 3)
        put(0, jnp.zeros((2 * block, block), jnp.float32))
        for j in (1, 2, 3):
            complete(1, j)
            if j > 1:
                complete(0, j)
            put(j, -(dot3(rows(0, j), first[...]) + dot3(rows(1, j), second[...])))

    @pl.when(z >= 2)
    def _():
        put(0, base(0))
        lower = colf[4:8].reshape(width, block) - dot3(
            cross[...].reshape(width, width), first[...]
        )
        second[...] = lower
        for i in range(2):
            out[2 + i] = second[pl.ds(pl.multiple_of((2 * i + r) * block, block), block), :]
        second[...] = dot3(gram[1], lower)
        first[...] = colf[0:4].reshape(width, block) - dot3(
            cross[...].reshape(width, width).T, second[...]
        )
        first[...] = dot3(gram[0], first[...])

        @pl.when(k == r)
        def _():
            for slot in (1, 2, 3):
                for m in (1, 3, 5, 7):
                    strip_wait(slots[slot], place(m))

        @pl.when(k != r)
        def _():
            for slot in range(4):
                for m in (0, 2, 4, 6):
                    strip_wait(slots[slot], place(m))

        both = jnp.concatenate([first[...].T, second[...].T], axis=1)
        for pair in range(2):
            strips = jnp.concatenate(
                [dcol[2 * pair + i].reshape(2 * width, block) for i in range(2)], axis=1
            )
            update = dot3(both, strips)
            for i in range(2):
                a = 4 + 2 * pair + i
                out[a] = mat[a] - update[:, i * block:(i + 1) * block].T

    @pl.when(z == 0)
    def _():
        for j in (1, 2, 0, 3):
            across(0, j)
        factor = fac[0, pl.ds(pl.multiple_of(own * block, block), block), :]
        for j in (1, 2, 0, 3):
            complete(0, j)
            put(j, dot3(rows(0, j), factor, 1))

    for q, j in chunks:
        @pl.when(active(q, j))
        def _():
            if climbs(q, j):
                @pl.when(rises(q, j))
                def _():
                    up_copy(q, j).wait_send()
            side_copy(q, j).wait_send()
            mate_copy(q, j, 0).wait_send()
            mate_copy(q, j, 1).wait_send()

    @pl.when(z >= 1)
    def _():
        for which in range(2):
            peer_copy(which).wait_send()
            oth_copy(which).wait_send()

    @pl.when(z >= 2)
    def _():
        for i in range(4):
            col_copy(i).wait_send()

    for even, condition in ((True, holder), (False, helper)):
        @pl.when(condition)
        def _():
            for slot in range(4):
                for m in range(8):
                    for way in ways(slot, m):
                        shared = slot == 0 and m % 2 == 1 and way == 2
                        if even == (m % 2 == 0 or shared):
                            strip_send_copy(slot, m, way).wait_send()


def panels(matrix, inverse_factors):
    row_blocks, block, _, _ = matrix.shape
    width = inverse_factors.shape[1]
    square = pltpu.VMEM((width, block), jnp.float32)
    dma = pltpu.SemaphoreType.DMA
    vmem = pl.BlockSpec(memory_space=pltpu.VMEM)
    result = pl.pallas_call(
        kernel,
        out_shape=jax.ShapeDtypeStruct((row_blocks, block, block), jnp.float32),
        in_specs=[pl.BlockSpec(memory_space=pltpu.HBM)] * 2,
        out_specs=vmem,
        scratch_shapes=[
            pltpu.VMEM((row_blocks, block, block), jnp.float32),
            pltpu.VMEM((2, width, width), jnp.float32),
            pltpu.VMEM((2, 4, row_blocks, block, block), jnp.float32),
            pltpu.VMEM((4, 2, block, block), jnp.float32),
            pltpu.VMEM((8, block, block), jnp.float32),
            pltpu.VMEM((4, 8, block, block), jnp.float32),
            pltpu.VMEM((4, block, width), jnp.float32),
            pltpu.VMEM((2, width, width), jnp.float32),
            square,
            square,
            dma((2, 4, 4)),
            dma((4,)),
            dma((4,)),
            dma((2, 4)),
            dma((2, 4)),
            dma((2, 4, 2)),
            dma((2, 2)),
            dma((4,)),
            dma((4, 8)),
            dma((4, 8, 3)),
            dma((2,)),
        ],
        compiler_params=pltpu.CompilerParams(
            collective_id=0, has_side_effects=True, vmem_limit_bytes=48 * 1024 * 1024
        ),
        cost_estimate=pl.CostEstimate(
            flops=2 * 10**9, bytes_accessed=4 * 2**20, transcendentals=0
        ),
    )(matrix.reshape(row_blocks, block, block), inverse_factors)
    return result.reshape(matrix.shape)


def solution(mesh):
    small = mesh.shape["col"] == 16 and mesh.shape["row"] == 2
    return jax.shard_map(
        panels if small else shards,
        mesh=mesh,
        in_specs=(P(None, "row", None, "col"), P()),
        out_specs=P(None, "row", None, "col"),
        check_vma=False,
    )
```

```python
import jax
import jax.numpy as jnp
from jax import lax
from jax.experimental import pallas as pl
from jax.experimental.pallas import tpu as pltpu
from jax.sharding import PartitionSpec as P


def broadcast(x, axis, root):
    mine = lax.axis_index(axis) == root
    return lax.psum(jnp.where(mine, x, jnp.zeros_like(x)), axis)


def exact_dot(left_side, right_side):
    return jnp.dot(
        left_side, right_side, precision=lax.Precision.HIGHEST, preferred_element_type=jnp.float32
    )


def shards(matrix, inverse_factors):
    col_count = lax.axis_size("col")
    row_count = lax.axis_size("row")
    col_index = lax.axis_index("col")
    row_index = lax.axis_index("row")
    row_blocks, block_cols, cycles, _ = matrix.shape
    panel_width = inverse_factors.shape[1]
    per_panel = panel_width // block_cols
    local_rows = row_blocks * block_cols
    square_view = matrix.reshape(local_rows, cycles * block_cols)
    global_rows = (
        (jnp.arange(row_blocks)[:, None] * row_count + row_index) * block_cols
        + jnp.arange(block_cols)[None, :]
    ).reshape(-1)
    take_index = (jnp.arange(cycles) * col_count + col_index) // row_count
    row_root = col_index % row_count

    def masked(factor_cols, offset):
        return jnp.where(global_rows[:, None] >= offset, factor_cols, 0.0)

    current = square_view
    for panel in range(2):
        factor = inverse_factors[panel]
        pieces = [
            broadcast(current, "col", panel * per_panel + member) for member in range(per_panel)
        ]
        factor_cols = exact_dot(jnp.concatenate(pieces, axis=1), factor.T)
        trailing = masked(factor_cols, (panel + 1) * panel_width)
        blocked = trailing.reshape(row_blocks, block_cols, panel_width)
        picked = jnp.take(blocked, take_index, axis=0).reshape(cycles * block_cols, panel_width)
        gathered = lax.all_gather(picked, "row", axis=0, tiled=True)
        column_part = lax.dynamic_slice_in_dim(
            gathered, row_root * picked.shape[0], picked.shape[0], 0
        )
        current = current - exact_dot(trailing, column_part.T)
        place_factor_cols = masked(factor_cols, panel * panel_width)
        offset_id = col_index - panel * per_panel
        inside = (offset_id >= 0) & (offset_id < per_panel)
        position = jnp.clip(offset_id, 0, per_panel - 1)
        chosen = lax.dynamic_slice_in_dim(place_factor_cols, position * block_cols, block_cols, 1)
        leading = jnp.where(inside, chosen, current)
        current = jnp.concatenate([leading, current[:, block_cols:]], axis=1)
    return current.reshape(row_blocks, block_cols, cycles, block_cols)


def split(value):
    high = value.astype(jnp.bfloat16)
    return high, (value - high.astype(jnp.float32)).astype(jnp.bfloat16)


def dot3(left_side, right_side, right_dim=0):
    left_high, left_low = split(left_side)
    right_high, right_low = split(right_side)

    def part(left, right):
        return lax.dot_general(
            left, right, (((1,), (right_dim,)), ((), ())), preferred_element_type=jnp.float32
        )

    return part(left_high, right_high) + (part(left_high, right_low) + part(left_low, right_high))


def kernel(
    mat_hbm, fac_hbm, out, mat, fac, pan, oth, colf, dcol, cross, gram, first, second,
    recv, oth_recv, col_recv, up_sem, side_sem, mate_sem, peer_sem, col_sem, strip_recv, strip_send, load_sem,
):
    c = lax.axis_index("col")
    r = lax.axis_index("row")
    z = c // 4
    x = (c // 2) % 2
    k = c % 2
    own = c % 4
    beside = own + 2 - 4 * x
    near = own + 1 - 2 * k
    far = beside + 1 - 2 * k
    up = {"col": c + 4, "row": r}
    down = {"col": c - 4, "row": r}
    side = {"col": c + 2 - 4 * x, "row": r}
    mate = {"col": c + 1 - 2 * k, "row": r}
    peer = {"col": c, "row": 1 - r}
    block = mat.shape[1]
    width = fac.shape[1]
    mesh_ids = pl.DeviceIdType.MESH

    def greet(device):
        pl.semaphore_signal(barrier, inc=1, device_id=device, device_id_type=mesh_ids)

    def copy(src, dst, send, receive, device):
        return pltpu.make_async_remote_copy(
            src_ref=src, dst_ref=dst, send_sem=send, recv_sem=receive,
            device_id=device, device_id_type=mesh_ids,
        )

    def active(q, j):
        if q == 0:
            return (z == 0, z >= 0, z < 2, z < 2)[j]
        return z == 1

    def rises(q, j):
        return z < 3 if j == 1 else z == 0

    def climbs(q, j):
        return q == 0 and j >= 1

    def strip(q, s, j):
        return pan.at[q, s, pl.ds(2 * j, 2)]

    def strip_copy(q, s, j, send, device):
        return copy(strip(q, s, j), strip(q, s, j), send, recv.at[q, s, j], device)

    def up_copy(q, j):
        return strip_copy(q, own, j, up_sem.at[q, j], up)

    def side_copy(q, j):
        return strip_copy(q, own, j, side_sem.at[q, j], side)

    def mate_copy(q, j, which):
        return strip_copy(q, (own, beside)[which], j, mate_sem.at[q, j, which], mate)

    def arrived(q, s, j):
        strip_copy(q, s, j, up_sem.at[q, j], mate).wait_recv()

    def peer_copy(which):
        s = (own, beside)[which]
        return copy(strip(0, s, 1), oth.at[s], peer_sem.at[0, which], oth_recv.at[s], peer)

    def oth_copy(which):
        s = (own, beside)[which]
        return copy(oth.at[s], oth.at[s], peer_sem.at[1, which], oth_recv.at[s], mate)

    def oth_arrived(s):
        copy(oth.at[s], oth.at[s], peer_sem.at[1, 0], oth_recv.at[s], mate).wait_recv()

    def col_copy(i):
        return copy(mat.at[i], colf.at[2 * i + r], col_sem.at[i], col_recv.at[i], peer)

    turn = 4 * (5 - 2 * z)
    turned = {"col": c + turn, "row": r}
    here = (z - 2) * 2 + x
    over = here + 1 - 2 * x
    ahead = here + turn // 2
    slots = (here, over, ahead, over + turn // 2)

    def place(m):
        return 2 * m + r if m < 4 else 2 * (m - 4) + 1 - r

    def strip_send_copy(slot, m, way, relayed=False):
        device = (side, turned, mate)[way]
        p = place(m)
        src = colf.at[p] if slot == 0 and not relayed else dcol.at[slots[slot], p]
        return copy(
            src, dcol.at[slots[slot], p], strip_send.at[slot, m, way],
            strip_recv.at[slots[slot], p], device,
        )

    def strip_wait(g, p):
        copy(
            dcol.at[g, p], dcol.at[g, p], strip_send.at[0, 0, 0], strip_recv.at[g, p], mate
        ).wait_recv()

    def ways(slot, m):
        if slot == 0:
            return (0, 1, 2)
        if slot == 1:
            return (1, 2) if m % 4 < 2 else (2,)
        if slot == 2:
            return (2,) if m % 4 < 2 else (0, 2)
        return (2,)

    holder = (z >= 2) & (k == r)
    lead = holder & (k == 1)
    giver = holder & (k == 0)
    relay = (z >= 2) & (k == 1) & (r == 0)
    taker = (z >= 2) & (k == 0) & (r == 1)

    def hand_on(slot, m, relayed):
        if slot > 0 or relayed:
            strip_wait(slots[slot], place(m))
        for way in ways(slot, m):
            if slot > 0 or not relayed or way < 2:
                strip_send_copy(slot, m, way, relayed).start()

    def carried(cases):
        for relayed, condition in ((False, lead), (True, relay)):
            @pl.when(condition)
            def _():
                for slot, m in cases:
                    hand_on(slot, m, relayed)

    def lane(q, j):
        @pl.when(active(q, j))
        def _():
            @pl.when(z != q)
            def _():
                arrived(q, own, j)

            if climbs(q, j):
                @pl.when(rises(q, j))
                def _():
                    up_copy(q, j).start()

            side_copy(q, j).start()
            mate_copy(q, j, 0).start()

    def across(q, j):
        @pl.when(active(q, j))
        def _():
            arrived(q, beside, j)
            mate_copy(q, j, 1).start()

    def complete(q, j):
        @pl.when(active(q, j))
        def _():
            arrived(q, near, j)
            arrived(q, far, j)

    def rows(q, j):
        half = [
            jnp.concatenate([pan[q, s, 2 * j + i] for s in range(4)], axis=1) for i in range(2)
        ]
        return jnp.concatenate(half, axis=0)

    def put(j, value):
        out[2 * j] = value[:block]
        out[2 * j + 1] = value[block:]

    def base(j):
        return jnp.concatenate([mat[2 * j], mat[2 * j + 1]], axis=0)

    mat_load = pltpu.make_async_copy(mat_hbm, mat, load_sem.at[0])
    fac_load = pltpu.make_async_copy(fac_hbm, fac, load_sem.at[1])
    mat_load.start()
    fac_load.start()

    barrier = pltpu.get_barrier_semaphore()
    greet(side)
    greet(mate)
    greet(peer)

    @pl.when(z < 3)
    def _():
        greet(up)

    @pl.when(z > 0)
    def _():
        greet(down)

    mat_load.wait()

    @pl.when(z >= 2)
    def _():
        for i in range(4):
            colf[2 * i + r] = mat[i]

    for q in range(2):
        @pl.when(z == q)
        def _():
            pan[q, own] = mat[...]

    between = (z > 0) & (z < 3)

    @pl.when(between)
    def _():
        pl.semaphore_wait(barrier, 5)

    @pl.when(jnp.logical_not(between))
    def _():
        pl.semaphore_wait(barrier, 4)

    chunks = [(1, 2), (0, 1), (1, 3), (0, 2), (0, 3), (1, 1), (0, 0)]

    @pl.when(z == 1)
    def _():
        lane(1, 2)
        lane(1, 3)
        lane(1, 1)

    @pl.when(z == 0)
    def _():
        lane(0, 1)
        lane(0, 2)
        lane(0, 0)
        lane(0, 3)

    @pl.when(z >= 2)
    def _():
        for i in range(4):
            col_copy(i).start()

    @pl.when(giver)
    def _():
        for m in range(4):
            strip_send_copy(0, m, 2).start()

    carried([(0, m) for m in range(4)])
    fac_load.wait()

    @pl.when(z >= 1)
    def _():
        gram[0] = dot3(fac[0].T, fac[0])
        @pl.when(z <= 2)
        def _():
            lane(0, 1)
            peer_copy(0).start()

        @pl.when(z >= 2)
        def _():
            for i in range(4):
                copy(
                    mat.at[i], colf.at[2 * i + 1 - r], col_sem.at[i], col_recv.at[i], peer
                ).wait_recv()

        @pl.when(giver)
        def _():
            for m in range(4, 8):
                strip_send_copy(0, m, 2).start()

        carried([(0, m) for m in range(4, 8)])
        carried([(slot, m) for m in range(4) for slot in (1, 2)])

        @pl.when(z == 3)
        def _():
            lane(0, 1)
            peer_copy(0).start()

        across(0, 1)
        peer_copy(1).start()

        @pl.when(z == 1)
        def _():
            lane(0, 2)


        @pl.when(z >= 2)
        def _():
            gram[1] = dot3(fac[1].T, fac[1])
            first[...] = dot3(gram[0], colf[0:4].reshape(width, block))

        oth_arrived(own)
        oth_copy(0).start()

        @pl.when(z == 1)
        def _():
            across(1, 2)
            across(1, 3)
            across(1, 1)
            lane(0, 3)

        oth_arrived(beside)
        oth_copy(1).start()

        @pl.when(z == 1)
        def _():
            across(0, 2)

        carried([(slot, m) for m in range(4, 8) for slot in (1, 2)])
        carried([(3, m) for m in range(8)])

        @pl.when(holder)
        def _():
            dcol[here] = colf[...]

        complete(0, 1)
        oth_arrived(near)
        oth_arrived(far)
        for i in range(2):
            for s in range(4):
                cross[2 * i + r, :, s * block:(s + 1) * block] = pan[0, s, 2 + i]
                cross[2 * i + 1 - r, :, s * block:(s + 1) * block] = oth[s, i]

    @pl.when(z == 1)
    def _():
        second[...] = -fac[1, pl.ds(pl.multiple_of(own * block, block), block), :].T
        first[...] = -dot3(cross[...].reshape(width, width).T, second[...])
        first[...] = dot3(gram[0], first[...])
        across(0, 3)
        put(0, jnp.zeros((2 * block, block), jnp.float32))
        for j in (1, 2, 3):
            complete(1, j)
            if j > 1:
                complete(0, j)
            put(j, -(dot3(rows(0, j), first[...]) + dot3(rows(1, j), second[...])))

    @pl.when(z >= 2)
    def _():
        put(0, base(0))
        lower = colf[4:8].reshape(width, block) - dot3(
            cross[...].reshape(width, width), first[...]
        )
        second[...] = lower
        for i in range(2):
            out[2 + i] = second[pl.ds(pl.multiple_of((2 * i + r) * block, block), block), :]
        second[...] = dot3(gram[1], lower)
        first[...] = colf[0:4].reshape(width, block) - dot3(
            cross[...].reshape(width, width).T, second[...]
        )
        first[...] = dot3(gram[0], first[...])

        @pl.when(k == 0)
        def _():
            for slot in (1, 2, 3):
                for m in range(8):
                    strip_wait(slots[slot], place(m))

        @pl.when(taker)
        def _():
            for m in range(8):
                strip_wait(here, place(m))

        both = jnp.concatenate([first[...].T, second[...].T], axis=1)
        for pair in range(2):
            strips = jnp.concatenate(
                [dcol[2 * pair + i].reshape(2 * width, block) for i in range(2)], axis=1
            )
            update = dot3(both, strips)
            for i in range(2):
                a = 4 + 2 * pair + i
                out[a] = mat[a] - update[:, i * block:(i + 1) * block].T

    @pl.when(z == 0)
    def _():
        for j in (1, 2, 0, 3):
            across(0, j)
        factor = fac[0, pl.ds(pl.multiple_of(own * block, block), block), :]
        for j in (1, 2, 0, 3):
            complete(0, j)
            put(j, dot3(rows(0, j), factor, 1))

    for q, j in chunks:
        @pl.when(active(q, j))
        def _():
            if climbs(q, j):
                @pl.when(rises(q, j))
                def _():
                    up_copy(q, j).wait_send()
            side_copy(q, j).wait_send()
            mate_copy(q, j, 0).wait_send()
            mate_copy(q, j, 1).wait_send()

    @pl.when(z >= 1)
    def _():
        for which in range(2):
            peer_copy(which).wait_send()
            oth_copy(which).wait_send()

    @pl.when(z >= 2)
    def _():
        for i in range(4):
            col_copy(i).wait_send()

    for relayed, condition in ((False, lead), (True, relay)):
        @pl.when(condition)
        def _():
            for slot in range(4):
                for m in range(8):
                    for way in ways(slot, m):
                        if slot > 0 or not relayed or way < 2:
                            strip_send_copy(slot, m, way, relayed).wait_send()

    @pl.when(giver)
    def _():
        for m in range(8):
            strip_send_copy(0, m, 2).wait_send()


def panels(matrix, inverse_factors):
    row_blocks, block, _, _ = matrix.shape
    width = inverse_factors.shape[1]
    square = pltpu.VMEM((width, block), jnp.float32)
    dma = pltpu.SemaphoreType.DMA
    vmem = pl.BlockSpec(memory_space=pltpu.VMEM)
    result = pl.pallas_call(
        kernel,
        out_shape=jax.ShapeDtypeStruct((row_blocks, block, block), jnp.float32),
        in_specs=[pl.BlockSpec(memory_space=pltpu.HBM)] * 2,
        out_specs=vmem,
        scratch_shapes=[
            pltpu.VMEM((row_blocks, block, block), jnp.float32),
            pltpu.VMEM((2, width, width), jnp.float32),
            pltpu.VMEM((2, 4, row_blocks, block, block), jnp.float32),
            pltpu.VMEM((4, 2, block, block), jnp.float32),
            pltpu.VMEM((8, block, block), jnp.float32),
            pltpu.VMEM((4, 8, block, block), jnp.float32),
            pltpu.VMEM((4, block, width), jnp.float32),
            pltpu.VMEM((2, width, width), jnp.float32),
            square,
            square,
            dma((2, 4, 4)),
            dma((4,)),
            dma((4,)),
            dma((2, 4)),
            dma((2, 4)),
            dma((2, 4, 2)),
            dma((2, 2)),
            dma((4,)),
            dma((4, 8)),
            dma((4, 8, 3)),
            dma((2,)),
        ],
        compiler_params=pltpu.CompilerParams(
            collective_id=0, has_side_effects=True, vmem_limit_bytes=48 * 1024 * 1024
        ),
        cost_estimate=pl.CostEstimate(
            flops=2 * 10**9, bytes_accessed=4 * 2**20, transcendentals=0
        ),
    )(matrix.reshape(row_blocks, block, block), inverse_factors)
    return result.reshape(matrix.shape)


def solution(mesh):
    small = mesh.shape["col"] == 16 and mesh.shape["row"] == 2
    return jax.shard_map(
        panels if small else shards,
        mesh=mesh,
        in_specs=(P(None, "row", None, "col"), P()),
        out_specs=P(None, "row", None, "col"),
        check_vma=False,
    )
```

```python
import jax
import jax.numpy as jnp
from jax import lax
from jax.experimental import pallas as pl
from jax.experimental.pallas import tpu as pltpu
from jax.sharding import PartitionSpec as P


def broadcast(x, axis, root):
    mine = lax.axis_index(axis) == root
    return lax.psum(jnp.where(mine, x, jnp.zeros_like(x)), axis)


def exact_dot(left_side, right_side):
    return jnp.dot(
        left_side, right_side, precision=lax.Precision.HIGHEST, preferred_element_type=jnp.float32
    )


def shards(matrix, inverse_factors):
    col_count = lax.axis_size("col")
    row_count = lax.axis_size("row")
    col_index = lax.axis_index("col")
    row_index = lax.axis_index("row")
    row_blocks, block_cols, cycles, _ = matrix.shape
    panel_width = inverse_factors.shape[1]
    per_panel = panel_width // block_cols
    local_rows = row_blocks * block_cols
    square_view = matrix.reshape(local_rows, cycles * block_cols)
    global_rows = (
        (jnp.arange(row_blocks)[:, None] * row_count + row_index) * block_cols
        + jnp.arange(block_cols)[None, :]
    ).reshape(-1)
    take_index = (jnp.arange(cycles) * col_count + col_index) // row_count
    row_root = col_index % row_count

    def masked(factor_cols, offset):
        return jnp.where(global_rows[:, None] >= offset, factor_cols, 0.0)

    current = square_view
    for panel in range(2):
        factor = inverse_factors[panel]
        pieces = [
            broadcast(current, "col", panel * per_panel + member) for member in range(per_panel)
        ]
        factor_cols = exact_dot(jnp.concatenate(pieces, axis=1), factor.T)
        trailing = masked(factor_cols, (panel + 1) * panel_width)
        blocked = trailing.reshape(row_blocks, block_cols, panel_width)
        picked = jnp.take(blocked, take_index, axis=0).reshape(cycles * block_cols, panel_width)
        gathered = lax.all_gather(picked, "row", axis=0, tiled=True)
        column_part = lax.dynamic_slice_in_dim(
            gathered, row_root * picked.shape[0], picked.shape[0], 0
        )
        current = current - exact_dot(trailing, column_part.T)
        place_factor_cols = masked(factor_cols, panel * panel_width)
        offset_id = col_index - panel * per_panel
        inside = (offset_id >= 0) & (offset_id < per_panel)
        position = jnp.clip(offset_id, 0, per_panel - 1)
        chosen = lax.dynamic_slice_in_dim(place_factor_cols, position * block_cols, block_cols, 1)
        leading = jnp.where(inside, chosen, current)
        current = jnp.concatenate([leading, current[:, block_cols:]], axis=1)
    return current.reshape(row_blocks, block_cols, cycles, block_cols)


def split(value):
    high = value.astype(jnp.bfloat16)
    return high, (value - high.astype(jnp.float32)).astype(jnp.bfloat16)


def dot3(left_side, right_side, right_dim=0):
    left_high, left_low = split(left_side)
    right_high, right_low = split(right_side)

    def part(left, right):
        return lax.dot_general(
            left, right, (((1,), (right_dim,)), ((), ())), preferred_element_type=jnp.float32
        )

    return part(left_high, right_high) + (part(left_high, right_low) + part(left_low, right_high))


def kernel(
    mat_hbm, fac_hbm, out, mat, fac, pan, oth, colf, dcol, cross, gram, first, second,
    recv, oth_recv, col_recv, up_sem, side_sem, mate_sem, peer_sem, col_sem, strip_recv, strip_send, load_sem,
):
    c = lax.axis_index("col")
    r = lax.axis_index("row")
    z = c // 4
    x = (c // 2) % 2
    k = c % 2
    own = c % 4
    beside = own + 2 - 4 * x
    near = own + 1 - 2 * k
    far = beside + 1 - 2 * k
    up = {"col": c + 4, "row": r}
    down = {"col": c - 4, "row": r}
    side = {"col": c + 2 - 4 * x, "row": r}
    mate = {"col": c + 1 - 2 * k, "row": r}
    peer = {"col": c, "row": 1 - r}
    block = mat.shape[1]
    width = fac.shape[1]
    mesh_ids = pl.DeviceIdType.MESH

    def greet(device):
        pl.semaphore_signal(barrier, inc=1, device_id=device, device_id_type=mesh_ids)

    def copy(src, dst, send, receive, device):
        return pltpu.make_async_remote_copy(
            src_ref=src, dst_ref=dst, send_sem=send, recv_sem=receive,
            device_id=device, device_id_type=mesh_ids,
        )

    def active(q, j):
        if q == 0:
            return (z == 0, z >= 0, z < 2, z < 2)[j]
        return z == 1

    def rises(q, j):
        return z < 3 if j == 1 else z == 0

    def climbs(q, j):
        return q == 0 and j >= 1

    def strip(q, s, j):
        return pan.at[q, s, pl.ds(2 * j, 2)]

    def strip_copy(q, s, j, send, device):
        return copy(strip(q, s, j), strip(q, s, j), send, recv.at[q, s, j], device)

    def up_copy(q, j):
        return strip_copy(q, own, j, up_sem.at[q, j], up)

    def side_copy(q, j):
        return strip_copy(q, own, j, side_sem.at[q, j], side)

    def mate_copy(q, j, which):
        return strip_copy(q, (own, beside)[which], j, mate_sem.at[q, j, which], mate)

    def arrived(q, s, j):
        strip_copy(q, s, j, up_sem.at[q, j], mate).wait_recv()

    def peer_copy(which):
        s = (own, beside)[which]
        return copy(strip(0, s, 1), oth.at[s], peer_sem.at[0, which], oth_recv.at[s], peer)

    def oth_copy(which):
        s = (own, beside)[which]
        return copy(oth.at[s], oth.at[s], peer_sem.at[1, which], oth_recv.at[s], mate)

    def oth_arrived(s):
        copy(oth.at[s], oth.at[s], peer_sem.at[1, 0], oth_recv.at[s], mate).wait_recv()

    def col_copy(i):
        return copy(mat.at[i], colf.at[2 * i + r], col_sem.at[i], col_recv.at[i], peer)

    turn = 4 * (5 - 2 * z)
    turned = {"col": c + turn, "row": r}
    here = (z - 2) * 2 + x
    over = here + 1 - 2 * x
    ahead = here + turn // 2
    slots = (here, over, ahead, over + turn // 2)

    def place(m):
        return 2 * m + r if m < 4 else 2 * (m - 4) + 1 - r

    def strip_send_copy(slot, m, way, relayed=False):
        device = (side, turned, mate)[way]
        p = place(m)
        src = colf.at[p] if slot == 0 and not relayed else dcol.at[slots[slot], p]
        return copy(
            src, dcol.at[slots[slot], p], strip_send.at[slot, m, way],
            strip_recv.at[slots[slot], p], device,
        )

    def strip_wait(g, p):
        copy(
            dcol.at[g, p], dcol.at[g, p], strip_send.at[0, 0, 0], strip_recv.at[g, p], mate
        ).wait_recv()

    def ways(slot, m):
        if slot == 0:
            return (0, 1, 2)
        if slot == 1:
            return (1, 2) if m % 4 < 2 else (2,)
        if slot == 2:
            return (2,) if m % 4 < 2 else (0, 2)
        return (2,)

    holder = (z >= 2) & (k == r)
    lead = holder & (k == 1)
    giver = holder & (k == 0)
    relay = (z >= 2) & (k == 1) & (r == 0)
    taker = (z >= 2) & (k == 0) & (r == 1)

    def hand_on(slot, m, relayed):
        if slot > 0 or relayed:
            strip_wait(slots[slot], place(m))
        for way in ways(slot, m):
            if slot > 0 or not relayed or way < 2:
                strip_send_copy(slot, m, way, relayed).start()

    def carried(cases):
        for relayed, condition in ((False, lead), (True, relay)):
            @pl.when(condition)
            def _():
                for slot, m in cases:
                    hand_on(slot, m, relayed)

    def lane(q, j):
        @pl.when(active(q, j))
        def _():
            @pl.when(z != q)
            def _():
                arrived(q, own, j)

            if climbs(q, j):
                @pl.when(rises(q, j))
                def _():
                    up_copy(q, j).start()

            side_copy(q, j).start()
            mate_copy(q, j, 0).start()

    def across(q, j):
        @pl.when(active(q, j))
        def _():
            arrived(q, beside, j)
            mate_copy(q, j, 1).start()

    def complete(q, j):
        @pl.when(active(q, j))
        def _():
            arrived(q, near, j)
            arrived(q, far, j)

    def rows(q, j):
        half = [
            jnp.concatenate([pan[q, s, 2 * j + i] for s in range(4)], axis=1) for i in range(2)
        ]
        return jnp.concatenate(half, axis=0)

    def put(j, value):
        out[2 * j] = value[:block]
        out[2 * j + 1] = value[block:]

    def base(j):
        return jnp.concatenate([mat[2 * j], mat[2 * j + 1]], axis=0)

    mat_load = pltpu.make_async_copy(mat_hbm, mat, load_sem.at[0])
    fac_load = pltpu.make_async_copy(fac_hbm, fac, load_sem.at[1])
    mat_load.start()
    fac_load.start()

    barrier = pltpu.get_barrier_semaphore()
    greet(side)
    greet(mate)
    greet(peer)

    @pl.when(z < 3)
    def _():
        greet(up)

    @pl.when(z > 0)
    def _():
        greet(down)

    mat_load.wait()

    @pl.when(z >= 2)
    def _():
        for i in range(4):
            colf[2 * i + r] = mat[i]

    for q in range(2):
        @pl.when(z == q)
        def _():
            pan[q, own] = mat[...]

    between = (z > 0) & (z < 3)

    @pl.when(between)
    def _():
        pl.semaphore_wait(barrier, 5)

    @pl.when(jnp.logical_not(between))
    def _():
        pl.semaphore_wait(barrier, 4)

    chunks = [(1, 2), (0, 1), (1, 3), (0, 2), (0, 3), (1, 1), (0, 0)]

    @pl.when(z == 1)
    def _():
        lane(1, 2)
        lane(1, 3)
        lane(1, 1)

    @pl.when(z == 0)
    def _():
        lane(0, 1)
        lane(0, 2)
        lane(0, 0)
        lane(0, 3)

    @pl.when(z >= 2)
    def _():
        for i in range(4):
            col_copy(i).start()

    @pl.when(giver)
    def _():
        for m in range(4):
            strip_send_copy(0, m, 2).start()

    carried([(0, m) for m in range(4)])
    fac_load.wait()

    @pl.when(z >= 1)
    def _():
        gram[0] = dot3(fac[0].T, fac[0])
        @pl.when(z <= 2)
        def _():
            lane(0, 1)
            peer_copy(0).start()

        @pl.when(z >= 2)
        def _():
            for i in range(4):
                copy(
                    mat.at[i], colf.at[2 * i + 1 - r], col_sem.at[i], col_recv.at[i], peer
                ).wait_recv()

        @pl.when(giver)
        def _():
            for m in range(4, 8):
                strip_send_copy(0, m, 2).start()

        carried([(0, m) for m in range(4, 8)])
        carried([(slot, m) for m in range(4) for slot in (1, 2)])

        @pl.when(z == 3)
        def _():
            lane(0, 1)
            peer_copy(0).start()

        carried([(slot, m) for m in range(4, 8) for slot in (1, 2)])
        across(0, 1)
        peer_copy(1).start()

        @pl.when(z == 1)
        def _():
            lane(0, 2)


        @pl.when(z >= 2)
        def _():
            gram[1] = dot3(fac[1].T, fac[1])
            first[...] = dot3(gram[0], colf[0:4].reshape(width, block))

        carried([(3, m) for m in range(4)])
        oth_arrived(own)
        oth_copy(0).start()

        @pl.when(z == 1)
        def _():
            across(1, 2)
            across(1, 3)
            across(1, 1)
            lane(0, 3)

        oth_arrived(beside)
        oth_copy(1).start()

        @pl.when(z == 1)
        def _():
            across(0, 2)

        carried([(3, m) for m in range(4, 8)])

        @pl.when(holder)
        def _():
            dcol[here] = colf[...]

        complete(0, 1)
        oth_arrived(near)
        oth_arrived(far)
        for i in range(2):
            for s in range(4):
                cross[2 * i + r, :, s * block:(s + 1) * block] = pan[0, s, 2 + i]
                cross[2 * i + 1 - r, :, s * block:(s + 1) * block] = oth[s, i]

    @pl.when(z == 1)
    def _():
        second[...] = -fac[1, pl.ds(pl.multiple_of(own * block, block), block), :].T
        first[...] = -dot3(cross[...].reshape(width, width).T, second[...])
        first[...] = dot3(gram[0], first[...])
        across(0, 3)
        put(0, jnp.zeros((2 * block, block), jnp.float32))
        for j in (1, 2, 3):
            complete(1, j)
            if j > 1:
                complete(0, j)
            put(j, -(dot3(rows(0, j), first[...]) + dot3(rows(1, j), second[...])))

    @pl.when(z >= 2)
    def _():
        put(0, base(0))
        lower = colf[4:8].reshape(width, block) - dot3(
            cross[...].reshape(width, width), first[...]
        )
        second[...] = lower
        for i in range(2):
            out[2 + i] = second[pl.ds(pl.multiple_of((2 * i + r) * block, block), block), :]
        second[...] = dot3(gram[1], lower)
        first[...] = colf[0:4].reshape(width, block) - dot3(
            cross[...].reshape(width, width).T, second[...]
        )
        first[...] = dot3(gram[0], first[...])

        @pl.when(k == 0)
        def _():
            for slot in (1, 2, 3):
                for m in range(8):
                    strip_wait(slots[slot], place(m))

        @pl.when(taker)
        def _():
            for m in range(8):
                strip_wait(here, place(m))

        both = jnp.concatenate([first[...].T, second[...].T], axis=1)
        for pair in range(2):
            strips = jnp.concatenate(
                [dcol[2 * pair + i].reshape(2 * width, block) for i in range(2)], axis=1
            )
            update = dot3(both, strips)
            for i in range(2):
                a = 4 + 2 * pair + i
                out[a] = mat[a] - update[:, i * block:(i + 1) * block].T

    @pl.when(z == 0)
    def _():
        for j in (1, 2, 0, 3):
            across(0, j)
        factor = fac[0, pl.ds(pl.multiple_of(own * block, block), block), :]
        for j in (1, 2, 0, 3):
            complete(0, j)
            put(j, dot3(rows(0, j), factor, 1))

    for q, j in chunks:
        @pl.when(active(q, j))
        def _():
            if climbs(q, j):
                @pl.when(rises(q, j))
                def _():
                    up_copy(q, j).wait_send()
            side_copy(q, j).wait_send()
            mate_copy(q, j, 0).wait_send()
            mate_copy(q, j, 1).wait_send()

    @pl.when(z >= 1)
    def _():
        for which in range(2):
            peer_copy(which).wait_send()
            oth_copy(which).wait_send()

    @pl.when(z >= 2)
    def _():
        for i in range(4):
            col_copy(i).wait_send()

    for relayed, condition in ((False, lead), (True, relay)):
        @pl.when(condition)
        def _():
            for slot in range(4):
                for m in range(8):
                    for way in ways(slot, m):
                        if slot > 0 or not relayed or way < 2:
                            strip_send_copy(slot, m, way, relayed).wait_send()

    @pl.when(giver)
    def _():
        for m in range(8):
            strip_send_copy(0, m, 2).wait_send()


def panels(matrix, inverse_factors):
    row_blocks, block, _, _ = matrix.shape
    width = inverse_factors.shape[1]
    square = pltpu.VMEM((width, block), jnp.float32)
    dma = pltpu.SemaphoreType.DMA
    vmem = pl.BlockSpec(memory_space=pltpu.VMEM)
    result = pl.pallas_call(
        kernel,
        out_shape=jax.ShapeDtypeStruct((row_blocks, block, block), jnp.float32),
        in_specs=[pl.BlockSpec(memory_space=pltpu.HBM)] * 2,
        out_specs=vmem,
        scratch_shapes=[
            pltpu.VMEM((row_blocks, block, block), jnp.float32),
            pltpu.VMEM((2, width, width), jnp.float32),
            pltpu.VMEM((2, 4, row_blocks, block, block), jnp.float32),
            pltpu.VMEM((4, 2, block, block), jnp.float32),
            pltpu.VMEM((8, block, block), jnp.float32),
            pltpu.VMEM((4, 8, block, block), jnp.float32),
            pltpu.VMEM((4, block, width), jnp.float32),
            pltpu.VMEM((2, width, width), jnp.float32),
            square,
            square,
            dma((2, 4, 4)),
            dma((4,)),
            dma((4,)),
            dma((2, 4)),
            dma((2, 4)),
            dma((2, 4, 2)),
            dma((2, 2)),
            dma((4,)),
            dma((4, 8)),
            dma((4, 8, 3)),
            dma((2,)),
        ],
        compiler_params=pltpu.CompilerParams(
            collective_id=0, has_side_effects=True, vmem_limit_bytes=48 * 1024 * 1024
        ),
        cost_estimate=pl.CostEstimate(
            flops=2 * 10**9, bytes_accessed=4 * 2**20, transcendentals=0
        ),
    )(matrix.reshape(row_blocks, block, block), inverse_factors)
    return result.reshape(matrix.shape)


def solution(mesh):
    small = mesh.shape["col"] == 16 and mesh.shape["row"] == 2
    return jax.shard_map(
        panels if small else shards,
        mesh=mesh,
        in_specs=(P(None, "row", None, "col"), P()),
        out_specs=P(None, "row", None, "col"),
        check_vma=False,
    )
```

```python
import jax
import jax.numpy as jnp
from jax import lax
from jax.experimental import pallas as pl
from jax.experimental.pallas import tpu as pltpu
from jax.sharding import PartitionSpec as P


def broadcast(x, axis, root):
    mine = lax.axis_index(axis) == root
    return lax.psum(jnp.where(mine, x, jnp.zeros_like(x)), axis)


def exact_dot(left_side, right_side):
    return jnp.dot(
        left_side, right_side, precision=lax.Precision.HIGHEST, preferred_element_type=jnp.float32
    )


def shards(matrix, inverse_factors):
    col_count = lax.axis_size("col")
    row_count = lax.axis_size("row")
    col_index = lax.axis_index("col")
    row_index = lax.axis_index("row")
    row_blocks, block_cols, cycles, _ = matrix.shape
    panel_width = inverse_factors.shape[1]
    per_panel = panel_width // block_cols
    local_rows = row_blocks * block_cols
    square_view = matrix.reshape(local_rows, cycles * block_cols)
    global_rows = (
        (jnp.arange(row_blocks)[:, None] * row_count + row_index) * block_cols
        + jnp.arange(block_cols)[None, :]
    ).reshape(-1)
    take_index = (jnp.arange(cycles) * col_count + col_index) // row_count
    row_root = col_index % row_count

    def masked(factor_cols, offset):
        return jnp.where(global_rows[:, None] >= offset, factor_cols, 0.0)

    current = square_view
    for panel in range(2):
        factor = inverse_factors[panel]
        pieces = [
            broadcast(current, "col", panel * per_panel + member) for member in range(per_panel)
        ]
        factor_cols = exact_dot(jnp.concatenate(pieces, axis=1), factor.T)
        trailing = masked(factor_cols, (panel + 1) * panel_width)
        blocked = trailing.reshape(row_blocks, block_cols, panel_width)
        picked = jnp.take(blocked, take_index, axis=0).reshape(cycles * block_cols, panel_width)
        gathered = lax.all_gather(picked, "row", axis=0, tiled=True)
        column_part = lax.dynamic_slice_in_dim(
            gathered, row_root * picked.shape[0], picked.shape[0], 0
        )
        current = current - exact_dot(trailing, column_part.T)
        place_factor_cols = masked(factor_cols, panel * panel_width)
        offset_id = col_index - panel * per_panel
        inside = (offset_id >= 0) & (offset_id < per_panel)
        position = jnp.clip(offset_id, 0, per_panel - 1)
        chosen = lax.dynamic_slice_in_dim(place_factor_cols, position * block_cols, block_cols, 1)
        leading = jnp.where(inside, chosen, current)
        current = jnp.concatenate([leading, current[:, block_cols:]], axis=1)
    return current.reshape(row_blocks, block_cols, cycles, block_cols)


def split(value):
    high = value.astype(jnp.bfloat16)
    return high, (value - high.astype(jnp.float32)).astype(jnp.bfloat16)


def dot3(left_side, right_side, right_dim=0):
    left_high, left_low = split(left_side)
    right_high, right_low = split(right_side)

    def part(left, right):
        return lax.dot_general(
            left, right, (((1,), (right_dim,)), ((), ())), preferred_element_type=jnp.float32
        )

    return part(left_high, right_high) + (part(left_high, right_low) + part(left_low, right_high))


def kernel(
    mat_hbm, fac_hbm, out, mat, fac, pan, oth, colf, dcol, cross, gram, first, second,
    recv, oth_recv, col_recv, up_sem, side_sem, mate_sem, peer_sem, col_sem, strip_recv, strip_send, load_sem,
):
    c = lax.axis_index("col")
    r = lax.axis_index("row")
    z = c // 4
    x = (c // 2) % 2
    k = c % 2
    own = c % 4
    beside = own + 2 - 4 * x
    near = own + 1 - 2 * k
    far = beside + 1 - 2 * k
    up = {"col": c + 4, "row": r}
    down = {"col": c - 4, "row": r}
    side = {"col": c + 2 - 4 * x, "row": r}
    mate = {"col": c + 1 - 2 * k, "row": r}
    peer = {"col": c, "row": 1 - r}
    block = mat.shape[1]
    width = fac.shape[1]
    mesh_ids = pl.DeviceIdType.MESH

    def greet(device):
        pl.semaphore_signal(barrier, inc=1, device_id=device, device_id_type=mesh_ids)

    def copy(src, dst, send, receive, device):
        return pltpu.make_async_remote_copy(
            src_ref=src, dst_ref=dst, send_sem=send, recv_sem=receive,
            device_id=device, device_id_type=mesh_ids,
        )

    def active(q, j):
        if q == 0:
            return (z == 0, z >= 0, z < 2, z < 2)[j]
        return z == 1

    def rises(q, j):
        return z < 3 if j == 1 else z == 0

    def climbs(q, j):
        return q == 0 and j >= 1

    def strip(q, s, j):
        return pan.at[q, s, pl.ds(2 * j, 2)]

    def strip_copy(q, s, j, send, device):
        return copy(strip(q, s, j), strip(q, s, j), send, recv.at[q, s, j], device)

    def up_copy(q, j):
        return strip_copy(q, own, j, up_sem.at[q, j], up)

    def side_copy(q, j):
        return strip_copy(q, own, j, side_sem.at[q, j], side)

    def mate_copy(q, j, which):
        return strip_copy(q, (own, beside)[which], j, mate_sem.at[q, j, which], mate)

    def arrived(q, s, j):
        strip_copy(q, s, j, up_sem.at[q, j], mate).wait_recv()

    def peer_copy(which):
        s = (own, beside)[which]
        return copy(strip(0, s, 1), oth.at[s], peer_sem.at[0, which], oth_recv.at[s], peer)

    def oth_copy(which):
        s = (own, beside)[which]
        return copy(oth.at[s], oth.at[s], peer_sem.at[1, which], oth_recv.at[s], mate)

    def oth_arrived(s):
        copy(oth.at[s], oth.at[s], peer_sem.at[1, 0], oth_recv.at[s], mate).wait_recv()

    def col_copy(i):
        return copy(mat.at[i], colf.at[2 * i + r], col_sem.at[i], col_recv.at[i], peer)

    turn = 4 * (5 - 2 * z)
    turned = {"col": c + turn, "row": r}
    here = (z - 2) * 2 + x
    over = here + 1 - 2 * x
    ahead = here + turn // 2
    slots = (here, over, ahead, over + turn // 2)

    def place(m):
        return 2 * m + r if m < 4 else 2 * (m - 4) + 1 - r

    def strip_send_copy(slot, m, way, relayed=False):
        device = (side, turned, mate)[way]
        p = place(m)
        src = colf.at[p] if slot == 0 and not relayed else dcol.at[slots[slot], p]
        return copy(
            src, dcol.at[slots[slot], p], strip_send.at[slot, m, way],
            strip_recv.at[slots[slot], p], device,
        )

    def strip_wait(g, p):
        copy(
            dcol.at[g, p], dcol.at[g, p], strip_send.at[0, 0, 0], strip_recv.at[g, p], mate
        ).wait_recv()

    def ways(slot, m):
        if slot == 0:
            return (0, 1, 2)
        if slot == 1:
            return (1, 2) if m % 4 < 2 else (2,)
        if slot == 2:
            return (2,) if m % 4 < 2 else (0, 2)
        return (2,)

    holder = (z >= 2) & (k == r)
    lead = holder & (k == 1)
    giver = holder & (k == 0)
    relay = (z >= 2) & (k == 1) & (r == 0)
    taker = (z >= 2) & (k == 0) & (r == 1)

    def hand_on(slot, m, relayed):
        if slot > 0 or relayed:
            strip_wait(slots[slot], place(m))
        for way in ways(slot, m):
            if slot > 0 or not relayed or way < 2:
                strip_send_copy(slot, m, way, relayed).start()

    def carried(cases):
        for relayed, condition in ((False, lead), (True, relay)):
            @pl.when(condition)
            def _():
                for slot, m in cases:
                    hand_on(slot, m, relayed)

    def lane(q, j):
        @pl.when(active(q, j))
        def _():
            @pl.when(z != q)
            def _():
                arrived(q, own, j)

            if climbs(q, j):
                @pl.when(rises(q, j))
                def _():
                    up_copy(q, j).start()

            side_copy(q, j).start()
            mate_copy(q, j, 0).start()

    def across(q, j):
        @pl.when(active(q, j))
        def _():
            arrived(q, beside, j)
            mate_copy(q, j, 1).start()

    def complete(q, j):
        @pl.when(active(q, j))
        def _():
            arrived(q, near, j)
            arrived(q, far, j)

    def rows(q, j):
        half = [
            jnp.concatenate([pan[q, s, 2 * j + i] for s in range(4)], axis=1) for i in range(2)
        ]
        return jnp.concatenate(half, axis=0)

    def put(j, value):
        out[2 * j] = value[:block]
        out[2 * j + 1] = value[block:]

    def base(j):
        return jnp.concatenate([mat[2 * j], mat[2 * j + 1]], axis=0)

    mat_load = pltpu.make_async_copy(mat_hbm, mat, load_sem.at[0])
    fac_load = pltpu.make_async_copy(fac_hbm, fac, load_sem.at[1])
    mat_load.start()
    fac_load.start()

    barrier = pltpu.get_barrier_semaphore()
    greet(side)
    greet(mate)
    greet(peer)

    @pl.when(z < 3)
    def _():
        greet(up)

    @pl.when(z > 0)
    def _():
        greet(down)

    mat_load.wait()

    @pl.when(z >= 2)
    def _():
        for i in range(4):
            colf[2 * i + r] = mat[i]

    for q in range(2):
        @pl.when(z == q)
        def _():
            pan[q, own] = mat[...]

    between = (z > 0) & (z < 3)

    @pl.when(between)
    def _():
        pl.semaphore_wait(barrier, 5)

    @pl.when(jnp.logical_not(between))
    def _():
        pl.semaphore_wait(barrier, 4)

    chunks = [(1, 2), (0, 1), (1, 3), (0, 2), (0, 3), (1, 1), (0, 0)]

    @pl.when(z == 1)
    def _():
        lane(1, 2)
        lane(1, 3)
        lane(1, 1)

    @pl.when(z == 0)
    def _():
        lane(0, 1)
        lane(0, 2)
        lane(0, 0)
        lane(0, 3)

    @pl.when(z >= 2)
    def _():
        for i in range(4):
            col_copy(i).start()

    @pl.when(giver)
    def _():
        for m in range(4):
            strip_send_copy(0, m, 2).start()

    carried([(0, m) for m in range(4)])
    fac_load.wait()

    @pl.when(z >= 1)
    def _():
        @pl.when(z <= 2)
        def _():
            lane(0, 1)
            peer_copy(0).start()

        gram[0] = dot3(fac[0].T, fac[0])

        @pl.when(z >= 2)
        def _():
            for i in range(4):
                copy(
                    mat.at[i], colf.at[2 * i + 1 - r], col_sem.at[i], col_recv.at[i], peer
                ).wait_recv()

        @pl.when(giver)
        def _():
            for m in range(4, 8):
                strip_send_copy(0, m, 2).start()

        carried([(0, m) for m in range(4, 8)])
        carried([(slot, m) for m in range(4) for slot in (1, 2)])

        @pl.when(z == 3)
        def _():
            lane(0, 1)
            peer_copy(0).start()

        carried([(slot, m) for m in range(4, 8) for slot in (1, 2)])
        across(0, 1)
        peer_copy(1).start()

        @pl.when(z == 1)
        def _():
            lane(0, 2)


        @pl.when(z >= 2)
        def _():
            gram[1] = dot3(fac[1].T, fac[1])
            first[...] = dot3(gram[0], colf[0:4].reshape(width, block))

        carried([(3, m) for m in range(4)])
        oth_arrived(own)
        oth_copy(0).start()

        @pl.when(z == 1)
        def _():
            across(1, 2)
            across(1, 3)
            across(1, 1)
            lane(0, 3)

        oth_arrived(beside)
        oth_copy(1).start()

        @pl.when(z == 1)
        def _():
            across(0, 2)

        carried([(3, m) for m in range(4, 8)])

        @pl.when(holder)
        def _():
            dcol[here] = colf[...]

        complete(0, 1)
        oth_arrived(near)
        oth_arrived(far)
        for i in range(2):
            for s in range(4):
                cross[2 * i + r, :, s * block:(s + 1) * block] = pan[0, s, 2 + i]
                cross[2 * i + 1 - r, :, s * block:(s + 1) * block] = oth[s, i]

    @pl.when(z == 1)
    def _():
        second[...] = -fac[1, pl.ds(pl.multiple_of(own * block, block), block), :].T
        first[...] = -dot3(cross[...].reshape(width, width).T, second[...])
        first[...] = dot3(gram[0], first[...])
        across(0, 3)
        put(0, jnp.zeros((2 * block, block), jnp.float32))
        for j in (1, 2, 3):
            complete(1, j)
            if j > 1:
                complete(0, j)
            put(j, -(dot3(rows(0, j), first[...]) + dot3(rows(1, j), second[...])))

    @pl.when(z >= 2)
    def _():
        put(0, base(0))
        lower = colf[4:8].reshape(width, block) - dot3(
            cross[...].reshape(width, width), first[...]
        )
        second[...] = lower
        for i in range(2):
            out[2 + i] = second[pl.ds(pl.multiple_of((2 * i + r) * block, block), block), :]
        second[...] = dot3(gram[1], lower)
        first[...] = colf[0:4].reshape(width, block) - dot3(
            cross[...].reshape(width, width).T, second[...]
        )
        first[...] = dot3(gram[0], first[...])

        @pl.when(k == 0)
        def _():
            for slot in (1, 2, 3):
                for m in range(8):
                    strip_wait(slots[slot], place(m))

        @pl.when(taker)
        def _():
            for m in range(8):
                strip_wait(here, place(m))

        both = jnp.concatenate([first[...].T, second[...].T], axis=1)
        for pair in range(2):
            strips = jnp.concatenate(
                [dcol[2 * pair + i].reshape(2 * width, block) for i in range(2)], axis=1
            )
            update = dot3(both, strips)
            for i in range(2):
                a = 4 + 2 * pair + i
                out[a] = mat[a] - update[:, i * block:(i + 1) * block].T

    @pl.when(z == 0)
    def _():
        for j in (1, 2, 0, 3):
            across(0, j)
        factor = fac[0, pl.ds(pl.multiple_of(own * block, block), block), :]
        for j in (1, 2, 0, 3):
            complete(0, j)
            put(j, dot3(rows(0, j), factor, 1))

    for q, j in chunks:
        @pl.when(active(q, j))
        def _():
            if climbs(q, j):
                @pl.when(rises(q, j))
                def _():
                    up_copy(q, j).wait_send()
            side_copy(q, j).wait_send()
            mate_copy(q, j, 0).wait_send()
            mate_copy(q, j, 1).wait_send()

    @pl.when(z >= 1)
    def _():
        for which in range(2):
            peer_copy(which).wait_send()
            oth_copy(which).wait_send()

    @pl.when(z >= 2)
    def _():
        for i in range(4):
            col_copy(i).wait_send()

    for relayed, condition in ((False, lead), (True, relay)):
        @pl.when(condition)
        def _():
            for slot in range(4):
                for m in range(8):
                    for way in ways(slot, m):
                        if slot > 0 or not relayed or way < 2:
                            strip_send_copy(slot, m, way, relayed).wait_send()

    @pl.when(giver)
    def _():
        for m in range(8):
            strip_send_copy(0, m, 2).wait_send()


def panels(matrix, inverse_factors):
    row_blocks, block, _, _ = matrix.shape
    width = inverse_factors.shape[1]
    square = pltpu.VMEM((width, block), jnp.float32)
    dma = pltpu.SemaphoreType.DMA
    vmem = pl.BlockSpec(memory_space=pltpu.VMEM)
    result = pl.pallas_call(
        kernel,
        out_shape=jax.ShapeDtypeStruct((row_blocks, block, block), jnp.float32),
        in_specs=[pl.BlockSpec(memory_space=pltpu.HBM)] * 2,
        out_specs=vmem,
        scratch_shapes=[
            pltpu.VMEM((row_blocks, block, block), jnp.float32),
            pltpu.VMEM((2, width, width), jnp.float32),
            pltpu.VMEM((2, 4, row_blocks, block, block), jnp.float32),
            pltpu.VMEM((4, 2, block, block), jnp.float32),
            pltpu.VMEM((8, block, block), jnp.float32),
            pltpu.VMEM((4, 8, block, block), jnp.float32),
            pltpu.VMEM((4, block, width), jnp.float32),
            pltpu.VMEM((2, width, width), jnp.float32),
            square,
            square,
            dma((2, 4, 4)),
            dma((4,)),
            dma((4,)),
            dma((2, 4)),
            dma((2, 4)),
            dma((2, 4, 2)),
            dma((2, 2)),
            dma((4,)),
            dma((4, 8)),
            dma((4, 8, 3)),
            dma((2,)),
        ],
        compiler_params=pltpu.CompilerParams(
            collective_id=0, has_side_effects=True, vmem_limit_bytes=48 * 1024 * 1024
        ),
        cost_estimate=pl.CostEstimate(
            flops=2 * 10**9, bytes_accessed=4 * 2**20, transcendentals=0
        ),
    )(matrix.reshape(row_blocks, block, block), inverse_factors)
    return result.reshape(matrix.shape)


def solution(mesh):
    small = mesh.shape["col"] == 16 and mesh.shape["row"] == 2
    return jax.shard_map(
        panels if small else shards,
        mesh=mesh,
        in_specs=(P(None, "row", None, "col"), P()),
        out_specs=P(None, "row", None, "col"),
        check_vma=False,
    )
```

```python
import jax
import jax.numpy as jnp
from jax import lax
from jax.experimental import pallas as pl
from jax.experimental.pallas import tpu as pltpu
from jax.sharding import PartitionSpec as P


def broadcast(x, axis, root):
    mine = lax.axis_index(axis) == root
    return lax.psum(jnp.where(mine, x, jnp.zeros_like(x)), axis)


def exact_dot(left_side, right_side):
    return jnp.dot(
        left_side, right_side, precision=lax.Precision.HIGHEST, preferred_element_type=jnp.float32
    )


def shards(matrix, inverse_factors):
    col_count = lax.axis_size("col")
    row_count = lax.axis_size("row")
    col_index = lax.axis_index("col")
    row_index = lax.axis_index("row")
    row_blocks, block_cols, cycles, _ = matrix.shape
    panel_width = inverse_factors.shape[1]
    per_panel = panel_width // block_cols
    local_rows = row_blocks * block_cols
    square_view = matrix.reshape(local_rows, cycles * block_cols)
    global_rows = (
        (jnp.arange(row_blocks)[:, None] * row_count + row_index) * block_cols
        + jnp.arange(block_cols)[None, :]
    ).reshape(-1)
    take_index = (jnp.arange(cycles) * col_count + col_index) // row_count
    row_root = col_index % row_count

    def masked(factor_cols, offset):
        return jnp.where(global_rows[:, None] >= offset, factor_cols, 0.0)

    current = square_view
    for panel in range(2):
        factor = inverse_factors[panel]
        pieces = [
            broadcast(current, "col", panel * per_panel + member) for member in range(per_panel)
        ]
        factor_cols = exact_dot(jnp.concatenate(pieces, axis=1), factor.T)
        trailing = masked(factor_cols, (panel + 1) * panel_width)
        blocked = trailing.reshape(row_blocks, block_cols, panel_width)
        picked = jnp.take(blocked, take_index, axis=0).reshape(cycles * block_cols, panel_width)
        gathered = lax.all_gather(picked, "row", axis=0, tiled=True)
        column_part = lax.dynamic_slice_in_dim(
            gathered, row_root * picked.shape[0], picked.shape[0], 0
        )
        current = current - exact_dot(trailing, column_part.T)
        place_factor_cols = masked(factor_cols, panel * panel_width)
        offset_id = col_index - panel * per_panel
        inside = (offset_id >= 0) & (offset_id < per_panel)
        position = jnp.clip(offset_id, 0, per_panel - 1)
        chosen = lax.dynamic_slice_in_dim(place_factor_cols, position * block_cols, block_cols, 1)
        leading = jnp.where(inside, chosen, current)
        current = jnp.concatenate([leading, current[:, block_cols:]], axis=1)
    return current.reshape(row_blocks, block_cols, cycles, block_cols)


def split(value):
    high = value.astype(jnp.bfloat16)
    return high, (value - high.astype(jnp.float32)).astype(jnp.bfloat16)


def dot3(left_side, right_side, right_dim=0):
    left_high, left_low = split(left_side)
    right_high, right_low = split(right_side)

    def part(left, right):
        return lax.dot_general(
            left, right, (((1,), (right_dim,)), ((), ())), preferred_element_type=jnp.float32
        )

    return part(left_high, right_high) + (part(left_high, right_low) + part(left_low, right_high))


def kernel(
    mat_hbm, fac_hbm, out, mat, fac, pan, oth, colf, dcol, cross, gram, first, second,
    recv, oth_recv, col_recv, up_sem, side_sem, mate_sem, peer_sem, col_sem, strip_recv, strip_send, load_sem,
):
    c = lax.axis_index("col")
    r = lax.axis_index("row")
    z = c // 4
    x = (c // 2) % 2
    k = c % 2
    own = c % 4
    beside = own + 2 - 4 * x
    near = own + 1 - 2 * k
    far = beside + 1 - 2 * k
    up = {"col": c + 4, "row": r}
    down = {"col": c - 4, "row": r}
    side = {"col": c + 2 - 4 * x, "row": r}
    mate = {"col": c + 1 - 2 * k, "row": r}
    peer = {"col": c, "row": 1 - r}
    block = mat.shape[1]
    width = fac.shape[1]
    mesh_ids = pl.DeviceIdType.MESH

    def greet(device):
        pl.semaphore_signal(barrier, inc=1, device_id=device, device_id_type=mesh_ids)

    def copy(src, dst, send, receive, device):
        return pltpu.make_async_remote_copy(
            src_ref=src, dst_ref=dst, send_sem=send, recv_sem=receive,
            device_id=device, device_id_type=mesh_ids,
        )

    def active(q, j):
        if q == 0:
            return (z == 0, z >= 0, z < 2, z < 2)[j]
        return z == 1

    def rises(q, j):
        return z < 3 if j == 1 else z == 0

    def climbs(q, j):
        return q == 0 and j >= 1

    def strip(q, s, j):
        return pan.at[q, s, pl.ds(2 * j, 2)]

    def strip_copy(q, s, j, send, device):
        return copy(strip(q, s, j), strip(q, s, j), send, recv.at[q, s, j], device)

    def up_copy(q, j):
        return strip_copy(q, own, j, up_sem.at[q, j], up)

    def side_copy(q, j):
        return strip_copy(q, own, j, side_sem.at[q, j], side)

    def mate_copy(q, j, which):
        return strip_copy(q, (own, beside)[which], j, mate_sem.at[q, j, which], mate)

    def arrived(q, s, j):
        strip_copy(q, s, j, up_sem.at[q, j], mate).wait_recv()

    def peer_copy(which):
        s = (own, beside)[which]
        return copy(strip(0, s, 1), oth.at[s], peer_sem.at[0, which], oth_recv.at[s], peer)

    def oth_copy(which):
        s = (own, beside)[which]
        return copy(oth.at[s], oth.at[s], peer_sem.at[1, which], oth_recv.at[s], mate)

    def oth_arrived(s):
        copy(oth.at[s], oth.at[s], peer_sem.at[1, 0], oth_recv.at[s], mate).wait_recv()

    def col_copy(i):
        return copy(mat.at[i], colf.at[2 * i + r], col_sem.at[i], col_recv.at[i], peer)

    turn = 4 * (5 - 2 * z)
    turned = {"col": c + turn, "row": r}
    here = (z - 2) * 2 + x
    over = here + 1 - 2 * x
    ahead = here + turn // 2
    slots = (here, over, ahead, over + turn // 2)

    def place(m):
        return 2 * m + r if m < 4 else 2 * (m - 4) + 1 - r

    def strip_send_copy(slot, m, way, relayed=False):
        device = (side, turned, mate)[way]
        p = place(m)
        src = colf.at[p] if slot == 0 and not relayed else dcol.at[slots[slot], p]
        return copy(
            src, dcol.at[slots[slot], p], strip_send.at[slot, m, way],
            strip_recv.at[slots[slot], p], device,
        )

    def strip_wait(g, p):
        copy(
            dcol.at[g, p], dcol.at[g, p], strip_send.at[0, 0, 0], strip_recv.at[g, p], mate
        ).wait_recv()

    def ways(slot, m):
        if slot == 0:
            return (0, 1, 2)
        if slot == 1:
            return (1, 2) if m % 4 < 2 else (2,)
        if slot == 2:
            return (2,) if m % 4 < 2 else (0, 2)
        return (2,)

    holder = (z >= 2) & (k == r)
    lead = holder & (k == 1)
    giver = holder & (k == 0)
    relay = (z >= 2) & (k == 1) & (r == 0)
    taker = (z >= 2) & (k == 0) & (r == 1)

    def hand_on(slot, m, relayed):
        if slot > 0 or relayed:
            strip_wait(slots[slot], place(m))
        for way in ways(slot, m):
            if slot > 0 or not relayed or way < 2:
                strip_send_copy(slot, m, way, relayed).start()

    def carried(cases):
        for relayed, condition in ((False, lead), (True, relay)):
            @pl.when(condition)
            def _():
                for slot, m in cases:
                    hand_on(slot, m, relayed)

    def lane(q, j):
        @pl.when(active(q, j))
        def _():
            @pl.when(z != q)
            def _():
                arrived(q, own, j)

            if climbs(q, j):
                @pl.when(rises(q, j))
                def _():
                    up_copy(q, j).start()

            side_copy(q, j).start()
            mate_copy(q, j, 0).start()

    def across(q, j):
        @pl.when(active(q, j))
        def _():
            arrived(q, beside, j)
            mate_copy(q, j, 1).start()

    def complete(q, j):
        @pl.when(active(q, j))
        def _():
            arrived(q, near, j)
            arrived(q, far, j)

    def rows(q, j):
        half = [
            jnp.concatenate([pan[q, s, 2 * j + i] for s in range(4)], axis=1) for i in range(2)
        ]
        return jnp.concatenate(half, axis=0)

    def put(j, value):
        out[2 * j] = value[:block]
        out[2 * j + 1] = value[block:]

    def base(j):
        return jnp.concatenate([mat[2 * j], mat[2 * j + 1]], axis=0)

    mat_load = pltpu.make_async_copy(mat_hbm, mat, load_sem.at[0])
    fac_load = pltpu.make_async_copy(fac_hbm, fac, load_sem.at[1])
    mat_load.start()
    fac_load.start()

    barrier = pltpu.get_barrier_semaphore()
    greet(side)
    greet(mate)
    greet(peer)

    @pl.when(z < 3)
    def _():
        greet(up)

    @pl.when(z > 0)
    def _():
        greet(down)

    mat_load.wait()

    @pl.when(z >= 2)
    def _():
        for i in range(4):
            colf[2 * i + r] = mat[i]

    for q in range(2):
        @pl.when(z == q)
        def _():
            pan[q, own] = mat[...]

    between = (z > 0) & (z < 3)

    @pl.when(between)
    def _():
        pl.semaphore_wait(barrier, 5)

    @pl.when(jnp.logical_not(between))
    def _():
        pl.semaphore_wait(barrier, 4)

    chunks = [(1, 2), (0, 1), (1, 3), (0, 2), (0, 3), (1, 1), (0, 0)]

    @pl.when(z == 1)
    def _():
        lane(1, 2)
        lane(1, 3)
        lane(1, 1)

    @pl.when(z == 0)
    def _():
        lane(0, 1)
        lane(0, 2)
        lane(0, 0)
        lane(0, 3)

    @pl.when(z >= 2)
    def _():
        for i in range(4):
            col_copy(i).start()

    @pl.when(giver)
    def _():
        for m in range(4):
            strip_send_copy(0, m, 2).start()

    carried([(0, m) for m in range(4)])
    fac_load.wait()

    @pl.when(z >= 1)
    def _():
        @pl.when(z <= 2)
        def _():
            lane(0, 1)
            peer_copy(0).start()

        gram[0] = dot3(fac[0].T, fac[0])

        @pl.when(z >= 2)
        def _():
            for i in range(4):
                copy(
                    mat.at[i], colf.at[2 * i + 1 - r], col_sem.at[i], col_recv.at[i], peer
                ).wait_recv()

        @pl.when(giver)
        def _():
            for m in range(4, 8):
                strip_send_copy(0, m, 2).start()

        carried([(0, m) for m in range(4, 8)])

        @pl.when(z == 3)
        def _():
            lane(0, 1)
            peer_copy(0).start()

        carried([(slot, m) for m in range(4) for slot in (1, 2)])

        carried([(slot, m) for m in range(4, 8) for slot in (1, 2)])
        across(0, 1)
        peer_copy(1).start()

        @pl.when(z == 1)
        def _():
            lane(0, 2)


        @pl.when(z >= 2)
        def _():
            gram[1] = dot3(fac[1].T, fac[1])
            first[...] = dot3(gram[0], colf[0:4].reshape(width, block))

        carried([(3, m) for m in range(4)])
        oth_arrived(own)
        oth_copy(0).start()

        @pl.when(z == 1)
        def _():
            across(1, 2)
            across(1, 3)
            across(1, 1)
            lane(0, 3)

        oth_arrived(beside)
        oth_copy(1).start()

        @pl.when(z == 1)
        def _():
            across(0, 2)

        carried([(3, m) for m in range(4, 8)])

        @pl.when(holder)
        def _():
            dcol[here] = colf[...]

        complete(0, 1)
        oth_arrived(near)
        oth_arrived(far)
        for i in range(2):
            for s in range(4):
                cross[2 * i + r, :, s * block:(s + 1) * block] = pan[0, s, 2 + i]
                cross[2 * i + 1 - r, :, s * block:(s + 1) * block] = oth[s, i]

    @pl.when(z == 1)
    def _():
        second[...] = -fac[1, pl.ds(pl.multiple_of(own * block, block), block), :].T
        first[...] = -dot3(cross[...].reshape(width, width).T, second[...])
        first[...] = dot3(gram[0], first[...])
        across(0, 3)
        put(0, jnp.zeros((2 * block, block), jnp.float32))
        for j in (1, 2, 3):
            complete(1, j)
            if j > 1:
                complete(0, j)
            put(j, -(dot3(rows(0, j), first[...]) + dot3(rows(1, j), second[...])))

    @pl.when(z >= 2)
    def _():
        put(0, base(0))
        lower = colf[4:8].reshape(width, block) - dot3(
            cross[...].reshape(width, width), first[...]
        )
        second[...] = lower
        for i in range(2):
            out[2 + i] = second[pl.ds(pl.multiple_of((2 * i + r) * block, block), block), :]
        second[...] = dot3(gram[1], lower)
        first[...] = colf[0:4].reshape(width, block) - dot3(
            cross[...].reshape(width, width).T, second[...]
        )
        first[...] = dot3(gram[0], first[...])

        @pl.when(k == 0)
        def _():
            for slot in (1, 2, 3):
                for m in range(8):
                    strip_wait(slots[slot], place(m))

        @pl.when(taker)
        def _():
            for m in range(8):
                strip_wait(here, place(m))

        both = jnp.concatenate([first[...].T, second[...].T], axis=1)
        for pair in range(2):
            strips = jnp.concatenate(
                [dcol[2 * pair + i].reshape(2 * width, block) for i in range(2)], axis=1
            )
            update = dot3(both, strips)
            for i in range(2):
                a = 4 + 2 * pair + i
                out[a] = mat[a] - update[:, i * block:(i + 1) * block].T

    @pl.when(z == 0)
    def _():
        for j in (1, 2, 0, 3):
            across(0, j)
        factor = fac[0, pl.ds(pl.multiple_of(own * block, block), block), :]
        for j in (1, 2, 0, 3):
            complete(0, j)
            put(j, dot3(rows(0, j), factor, 1))

    for q, j in chunks:
        @pl.when(active(q, j))
        def _():
            if climbs(q, j):
                @pl.when(rises(q, j))
                def _():
                    up_copy(q, j).wait_send()
            side_copy(q, j).wait_send()
            mate_copy(q, j, 0).wait_send()
            mate_copy(q, j, 1).wait_send()

    @pl.when(z >= 1)
    def _():
        for which in range(2):
            peer_copy(which).wait_send()
            oth_copy(which).wait_send()

    @pl.when(z >= 2)
    def _():
        for i in range(4):
            col_copy(i).wait_send()

    for relayed, condition in ((False, lead), (True, relay)):
        @pl.when(condition)
        def _():
            for slot in range(4):
                for m in range(8):
                    for way in ways(slot, m):
                        if slot > 0 or not relayed or way < 2:
                            strip_send_copy(slot, m, way, relayed).wait_send()

    @pl.when(giver)
    def _():
        for m in range(8):
            strip_send_copy(0, m, 2).wait_send()


def panels(matrix, inverse_factors):
    row_blocks, block, _, _ = matrix.shape
    width = inverse_factors.shape[1]
    square = pltpu.VMEM((width, block), jnp.float32)
    dma = pltpu.SemaphoreType.DMA
    vmem = pl.BlockSpec(memory_space=pltpu.VMEM)
    result = pl.pallas_call(
        kernel,
        out_shape=jax.ShapeDtypeStruct((row_blocks, block, block), jnp.float32),
        in_specs=[pl.BlockSpec(memory_space=pltpu.HBM)] * 2,
        out_specs=vmem,
        scratch_shapes=[
            pltpu.VMEM((row_blocks, block, block), jnp.float32),
            pltpu.VMEM((2, width, width), jnp.float32),
            pltpu.VMEM((2, 4, row_blocks, block, block), jnp.float32),
            pltpu.VMEM((4, 2, block, block), jnp.float32),
            pltpu.VMEM((8, block, block), jnp.float32),
            pltpu.VMEM((4, 8, block, block), jnp.float32),
            pltpu.VMEM((4, block, width), jnp.float32),
            pltpu.VMEM((2, width, width), jnp.float32),
            square,
            square,
            dma((2, 4, 4)),
            dma((4,)),
            dma((4,)),
            dma((2, 4)),
            dma((2, 4)),
            dma((2, 4, 2)),
            dma((2, 2)),
            dma((4,)),
            dma((4, 8)),
            dma((4, 8, 3)),
            dma((2,)),
        ],
        compiler_params=pltpu.CompilerParams(
            collective_id=0, has_side_effects=True, vmem_limit_bytes=48 * 1024 * 1024
        ),
        cost_estimate=pl.CostEstimate(
            flops=2 * 10**9, bytes_accessed=4 * 2**20, transcendentals=0
        ),
    )(matrix.reshape(row_blocks, block, block), inverse_factors)
    return result.reshape(matrix.shape)


def solution(mesh):
    small = mesh.shape["col"] == 16 and mesh.shape["row"] == 2
    return jax.shard_map(
        panels if small else shards,
        mesh=mesh,
        in_specs=(P(None, "row", None, "col"), P()),
        out_specs=P(None, "row", None, "col"),
        check_vma=False,
    )
```
